256 devices in a mesh: seq: 32 (over z, y), ch: 8 (over x, core).
Axes of the slice: x: 4, y: 4, z: 8, core: 2. Of those that a mesh axis runs over, the one named last changes fastest.
Arguments:
- q_proj: bfloat16 [16384, 4096], P('seq', 'ch'), may hold values from -6 to 6
- k_proj: bfloat16 [16384, 4096], P('seq', 'ch'), may hold values from -6 to 6
- v_proj: bfloat16 [16384, 4096], P('seq', 'ch'), may hold values from -6 to 6
- short_weight: float32 [3, 3, 4096], P(None, None, 'ch'), may hold values from -3 to 3
- long_filter: bfloat16 [16384, 4096], P('seq', 'ch'), may hold values from -0.046875 to 0.046875
- long_bias: float32 [4096], P('ch'), may hold values from -4 to 4
- residual: bfloat16 [16384, 4096], P('seq', 'ch'), may hold values from -400 to 400
- norm_gain: float32 [4096], P('ch'), may hold values from 0.1 to 1.9
Outputs:
- stream: bfloat16 [16384, 4096], P('seq', 'ch')
- normed: bfloat16 [16384, 4096], P('seq', 'ch')
The draws below stay inside these ranges and needn't reach their ends.
All inputs are finite; a program needn't handle non-finite values.
Results may differ from the reference program's by a relative error of at most 0.011.
Values may be sent and summed in bfloat16 or wider, within the bound.
A program may use at most 128 MiB of HBM per device.

```python
import math
import jax
import jax.numpy as jnp
from jax import lax

D = 4096
TAPS = 3
TOKENS = 16384


def draw_residual(key, part):
    key = jax.random.fold_in(key, 11)
    key_rows, key_cols, key_base = jax.random.split(key, 3)
    row_scale = jnp.exp(jax.random.uniform(key_rows, (TOKENS, 1), jnp.float32, math.log(0.5), math.log(5.0)))
    ramp = jnp.power(3.0, jnp.arange(D, dtype=jnp.float32)[None, :] / D)
    col_scale = 0.5 * ramp * jnp.exp(jax.random.uniform(key_cols, (1, D), jnp.float32, 0.0, math.log(3.3)))
    base = jax.random.normal(key_base, (TOKENS, D), jnp.float32)
    return (base * row_scale * col_scale).astype(jnp.bfloat16)


def levels(rng, shape, shards, low, largest):
    level = 1.0
    for dim, blocks in shards:
        steps = jax.random.uniform(jax.random.fold_in(jax.random.fold_in(rng, 6), dim), (blocks,), jnp.float32, low / len(shards), largest / len(shards))
        level = level * jnp.repeat(jnp.exp(steps), shape[dim] // blocks).reshape((-1,) + (1,) * (len(shape) - 1 - dim))
    return level


def centred(own_key, extent, width, most, cuts=(), kind=jnp.bfloat16):
    loudness = levels(own_key, extent, cuts, -0.22, 0.18) if cuts else 1.0
    array = jax.random.normal(own_key, extent, jnp.float32) * width * loudness
    return jnp.minimum(jnp.maximum(array, -most), most).astype(kind)


def setup_inputs(seed: int = 0) -> dict:
    streams_of = jax.random.split(jax.random.key(seed), 9)
    q_proj = centred(streams_of[0], (TOKENS, D), 1.0, 6.0, ((0, 32), (1, 8)))
    k_proj = centred(streams_of[1], (TOKENS, D), 1.0, 6.0, ((0, 32), (1, 8)))
    v_proj = centred(streams_of[2], (TOKENS, D), 1.0, 6.0, ((0, 32), (1, 8)))
    short_weight = centred(streams_of[3], (3, TAPS, D), 0.6, 3.0, ((2, 8),), jnp.float32)
    long_filter = centred(streams_of[4], (TOKENS, D), TOKENS ** -0.5, 0.046875, ((0, 32), (1, 8)))
    long_bias = centred(streams_of[5], (D,), 1.0, 4.0, ((0, 8),), jnp.float32)
    residual = draw_residual(jax.random.fold_in(streams_of[8], 71), 0)
    norm_gain = jnp.clip(1.0 + 0.18 * jax.random.normal(streams_of[7], (D,), jnp.float32), 0.1, 1.9)
    return {"q_proj": q_proj, "k_proj": k_proj, "v_proj": v_proj, "short_weight": short_weight, "long_filter": long_filter, "long_bias": long_bias, "residual": residual, "norm_gain": norm_gain}


def reference(q_proj, k_proj, v_proj, short_weight, long_filter, long_bias, residual, norm_gain):
    length = q_proj.shape[0]
    streams = jnp.stack([q_proj, k_proj, v_proj]).astype(jnp.float32)
    padded = jnp.pad(streams, ((0, 0), (TAPS - 1, 0), (0, 0)))
    filtered = sum((short_weight[:, lag_index, None, :] * padded[:, TAPS - 1 - lag_index:TAPS - 1 - lag_index + length, :] for lag_index in range(TAPS)))
    pregate = (filtered[1] * filtered[2]).astype(jnp.bfloat16)
    block_width = math.gcd(D, 512)
    block_count = D // block_width
    zero_blocks = pregate.astype(jnp.float32).reshape(length, block_count, block_width).transpose(1, 0, 2)
    filter_blocks = long_filter.astype(jnp.float32).reshape(length, block_count, block_width).transpose(1, 0, 2)

    def convolve(pair):
        signal, taps_block = pair
        spectrum = jnp.fft.rfft(signal, n=2 * length, axis=0) * jnp.fft.rfft(taps_block, n=2 * length, axis=0)
        return jnp.fft.irfft(spectrum, n=2 * length, axis=0)[:length]
    conv = lax.map(convolve, (zero_blocks, filter_blocks)).transpose(1, 0, 2).reshape(length, D)
    mixed = (filtered[0] * (conv + long_bias * pregate.astype(jnp.float32))).astype(jnp.bfloat16)
    mixed = lax.optimization_barrier(mixed)
    stream = (residual.astype(jnp.float32) + mixed.astype(jnp.float32)).astype(jnp.bfloat16)
    values = stream.astype(jnp.float32)
    power = lax.optimization_barrier(jnp.sum(values * values, axis=1)) / D
    normed = (values * lax.rsqrt(power + 1e-06)[:, None] * norm_gain).astype(jnp.bfloat16)
    return (stream, normed)
```

```python
import functools
import math

import jax
import jax.numpy as jnp
import ml_dtypes
import numpy as np
from jax import lax
from jax.experimental import pallas as pl
from jax.experimental.pallas import tpu as pltpu
from jax.sharding import PartitionSpec as P

D = 4096
MESH = pl.DeviceIdType.MESH
F32 = jnp.float32
BF16 = jnp.bfloat16
LANES = 128


def tables(pieces):
    n = LANES
    quarter = np.arange(n) + 0.25
    per = n // pieces
    rows = np.array([per * (r % pieces) + r // pieces for r in range(n)])
    angle = 2 * math.pi / n * (quarter[:, None] * rows[None, :] % n)
    first = np.concatenate([np.cos(angle), -np.sin(angle)], axis=0)
    last = np.concatenate([np.cos(angle.T), -np.sin(angle.T)], axis=1) / (n * n)
    points = np.arange(n)
    angle = 2 * math.pi / n * (points[:, None] * points[None, :] % n)
    cosine, sine = np.cos(angle), np.sin(angle)
    second = np.block([[cosine, -sine], [sine, cosine]])
    angle = 2 * math.pi / (n * n) * (quarter[:, None] * points[None, :])
    return (
        first.astype(ml_dtypes.bfloat16),
        second.astype(ml_dtypes.bfloat16),
        second.T.copy().astype(ml_dtypes.bfloat16),
        last.astype(ml_dtypes.bfloat16),
        np.cos(angle).astype(np.float32),
        np.sin(angle).astype(np.float32),
    )


def dot(left, right):
    return jnp.dot(left, right, preferred_element_type=F32)


def kernel(
    pieces,
    groups,
    q_in, k_in, v_in, h_in, res_in, taps_in, bias_in, gain_in,
    first_in, second_in, third_in, last_in, cos_in, sin_in,
    stream_out, normed_out,
    q_b, k_b, v_b, h_b, res_b, taps, bias, gain,
    first, second, third, last, cos_t, sin_t,
    pad_q, pad_k, pad_v, halo_out, halo_in,
    h_send, z_send, y_send, h_recv, z_recv, y_recv,
    gate_t, skip_t, res_t, flat, spectrum_h, product, power_slots, normed_b, stream_b,
    load_sem, halo_sem, send_sem, recv_sem, power_sem, store_sem,
):
    me, ch = lax.axis_index("seq"), lax.axis_index("ch")
    tokens, channels = h_b.shape
    own = channels // pieces
    blocks = tokens // LANES
    wide = channels // LANES

    barrier = pltpu.get_barrier_semaphore()

    def greet(d, _):
        pl.semaphore_signal(barrier, inc=1, device_id=(lax.rem(me + d, pieces), ch), device_id_type=MESH)
        return 0

    lax.fori_loop(1, pieces, greet, 0)

    def greet_row(d, _):
        pl.semaphore_signal(barrier, inc=1, device_id=(me, lax.rem(ch + d, groups)), device_id_type=MESH)
        return 0

    lax.fori_loop(1, groups, greet_row, 0)

    pairs = [
        (h_in, h_b), (q_in, q_b), (k_in, k_b), (v_in, v_b), (taps_in, taps), (bias_in, bias), (first_in, first),
        (second_in, second), (third_in, third), (last_in, last), (cos_in, cos_t), (sin_in, sin_t),
        (res_in, res_b), (gain_in, gain),
    ]
    loads = [pltpu.make_async_copy(src, dst, load_sem.at[i]) for i, (src, dst) in enumerate(pairs)]
    for load in loads:
        load.start()

    loads[0].wait()
    for r in range(blocks):
        for c in range(wide):
            tile = h_b[r * LANES : (r + 1) * LANES, c * LANES : (c + 1) * LANES]
            h_send[c * LANES : (c + 1) * LANES, r * LANES : (r + 1) * LANES] = tile.T

    for i in (1, 2, 3):
        loads[i].wait()
    tails = [x[tokens - 16 :, :].astype(F32)[14:, :] for x in (q_b, k_b, v_b)]
    halo_out[...] = jnp.concatenate(tails + [jnp.zeros((2, channels), F32)], axis=0)

    pl.semaphore_wait(barrier, pieces - 1 + groups - 1)

    halo_copy = pltpu.make_async_remote_copy(
        src_ref=halo_out, dst_ref=halo_in, send_sem=halo_sem.at[0], recv_sem=halo_sem.at[1],
        device_id=(lax.rem(me + 1, pieces), ch), device_id_type=MESH,
    )

    @pl.when(me < pieces - 1)
    def _():
        halo_copy.start()

    def send_all(source, target, slot):
        def send(d, _):
            other = lax.rem(me + d, pieces)
            pltpu.make_async_remote_copy(
                src_ref=source.at[pl.ds(pl.multiple_of(other * own, own), own)],
                dst_ref=target.at[pl.ds(pl.multiple_of(me * own, own), own)],
                send_sem=send_sem.at[slot], recv_sem=recv_sem.at[slot],
                device_id=(other, ch), device_id_type=MESH,
            ).start()
            return 0

        lax.fori_loop(1, pieces, send, 0)
        mine = pl.ds(pl.multiple_of(me * own, own), own)
        pltpu.make_async_copy(source.at[mine], target.at[mine], recv_sem.at[slot]).start()

    def wait_recv(target, slot):
        pltpu.make_async_copy(target, target, recv_sem.at[slot]).wait()

    def wait_send(source, slot):
        part = source.at[pl.ds(0, channels - own)]
        pltpu.make_async_copy(part, part, send_sem.at[slot]).wait()

    send_all(h_send, h_recv, 0)

    @pl.when(me == 0)
    def _():
        halo_in[...] = jnp.zeros_like(halo_in)

    for x, padded in ((q_b, pad_q), (k_b, pad_k), (v_b, pad_v)):
        padded[8:, :] = x[...].astype(F32)

    @pl.when(me > 0)
    def _():
        halo_copy.wait_recv()

    @pl.when(me < pieces - 1)
    def _():
        halo_copy.wait_send()

    for i, padded in enumerate((pad_q, pad_k, pad_v)):
        padded[6:8, :] = halo_in[2 * i : 2 * i + 2, :]

    for i in (4, 5):
        loads[i].wait()

    for r in range(blocks):
        for c in range(wide):
            cols = slice(c * LANES, (c + 1) * LANES)
            rows = slice(r * LANES, (r + 1) * LANES)

            def short(s, padded):
                total = taps[s, 0:1, cols] * padded[8 + r * LANES : 8 + (r + 1) * LANES, cols]
                total += taps[s, 1:2, cols] * padded[7 + r * LANES : 7 + (r + 1) * LANES, cols]
                return total + taps[s, 2:3, cols] * padded[6 + r * LANES : 6 + (r + 1) * LANES, cols]

            pregate = (short(1, pad_k) * short(2, pad_v)).astype(BF16)
            z_send[cols, rows] = pregate.T
            gate_t[cols, rows] = short(0, pad_q).T
            skip_t[cols, rows] = (pregate.astype(F32) * bias[0:1, cols]).T

    send_all(z_send, z_recv, 1)

    loads[12].wait()
    for r in range(blocks):
        for c in range(wide):
            cols = slice(c * LANES, (c + 1) * LANES)
            rows = slice(r * LANES, (r + 1) * LANES)
            res_t[cols, rows] = res_b[rows, cols].T.astype(F32)

    for i in (6, 7, 8, 9, 10, 11, 13):
        loads[i].wait()

    def forward(received, p):
        signal = [
            jnp.concatenate(
                [flat[i, pl.ds(2 * p + e, pieces, stride=own), :] for i in range(blocks)], axis=0
            )
            for e in range(2)
        ]
        signal = jnp.concatenate(signal, axis=1).astype(BF16)
        partial = dot(first[...], signal)
        turned = []
        for e in range(2):
            real = partial[:LANES, e * LANES : (e + 1) * LANES]
            imag = partial[LANES:, e * LANES : (e + 1) * LANES]
            cosine, sine = cos_t[...], sin_t[...]
            turned.append(
                jnp.concatenate([real * cosine + imag * sine, imag * cosine - real * sine], axis=1).astype(BF16)
            )
        return dot(jnp.concatenate(turned, axis=0), second[...])

    def widen(received):
        def step(r, _):
            rows = pl.ds(pl.multiple_of(r * 64, 64), 64)
            for i in range(blocks):
                flat[i, rows, :] = received[rows, i * LANES : (i + 1) * LANES].astype(F32)
            return 0

        lax.fori_loop(0, channels // 64, step, 0)

    wait_recv(h_recv, 0)
    widen(h_recv)

    def filter_step(p, _):
        spectrum_h[pl.ds(pl.multiple_of(p * 256, 256), 256), :] = forward(h_recv, p)
        return 0

    lax.fori_loop(0, own // 2, filter_step, 0)

    wait_recv(z_recv, 1)
    widen(z_recv)

    def signal_step(p, _):
        x = forward(z_recv, p)
        w = spectrum_h[pl.ds(pl.multiple_of(p * 256, 256), 256), :]
        xr, xi, wr, wi = x[:, :LANES], x[:, LANES:], w[:, :LANES], w[:, LANES:]
        both = jnp.concatenate([xr * wr - xi * wi, xr * wi + xi * wr], axis=1).astype(BF16)
        back = dot(both, third[...])
        turned = []
        for e in range(2):
            real = back[e * LANES : (e + 1) * LANES, :LANES]
            imag = back[e * LANES : (e + 1) * LANES, LANES:]
            cosine, sine = cos_t[...], sin_t[...]
            turned.append(
                jnp.concatenate([real * cosine - imag * sine, real * sine + imag * cosine], axis=0).astype(BF16)
            )
        result = dot(last[...], jnp.concatenate(turned, axis=1))
        for e in range(2):
            for i in range(blocks):
                product[i, pl.ds(2 * p + e, pieces, stride=own), :] = result[
                    i * pieces : (i + 1) * pieces, e * LANES : (e + 1) * LANES
                ]
        return 0

    lax.fori_loop(0, own // 2, signal_step, 0)

    def narrow(r, _):
        rows = pl.ds(pl.multiple_of(r * 64, 64), 64)
        for i in range(blocks):
            y_send[rows, i * LANES : (i + 1) * LANES] = product[i, rows, :].astype(BF16)
        return 0

    lax.fori_loop(0, channels // 64, narrow, 0)
    send_all(y_send, y_recv, 2)

    wait_recv(y_recv, 2)

    def gate_step(r, total):
        rows = pl.ds(pl.multiple_of(r * 32, 32), 32)
        mixed = (gate_t[rows, :] * (y_recv[rows, :].astype(F32) + skip_t[rows, :])).astype(BF16)
        stream = (res_t[rows, :] + mixed.astype(F32)).astype(BF16).astype(F32)
        res_t[rows, :] = stream
        squares = stream * stream
        return total + ((squares[0:8] + squares[8:16]) + (squares[16:24] + squares[24:32]))

    total = lax.fori_loop(0, channels // 32, gate_step, jnp.zeros((8, tokens), F32))
    power_slots[ch] = jnp.sum(total, axis=0, keepdims=True)

    def power_copy(d):
        other = lax.rem(ch + d, groups)
        return pltpu.make_async_remote_copy(
            src_ref=power_slots.at[ch], dst_ref=power_slots.at[ch],
            send_sem=power_sem.at[0], recv_sem=power_sem.at[1],
            device_id=(me, other), device_id_type=MESH,
        )

    for d in range(1, groups):
        power_copy(d).start()

    for r in range(blocks):
        for c in range(wide):
            cols = slice(c * LANES, (c + 1) * LANES)
            rows = slice(r * LANES, (r + 1) * LANES)
            stream_b[rows, cols] = res_t[cols, rows].T.astype(BF16)
    stream_copy = pltpu.make_async_copy(stream_b, stream_out, store_sem.at[0])
    stream_copy.start()

    part = power_slots.at[pl.ds(0, groups - 1)]
    pltpu.make_async_copy(part, part, power_sem.at[1]).wait()
    power = jnp.sum(power_slots[...], axis=0) / D
    scale = lax.rsqrt(power + 1e-6)
    for r in range(blocks):
        rows = slice(r * LANES, (r + 1) * LANES)
        column = jnp.broadcast_to(scale[:, rows], (LANES, LANES)).T
        for c in range(wide):
            cols = slice(c * LANES, (c + 1) * LANES)
            normed_b[rows, cols] = (stream_b[rows, cols].astype(F32) * column * gain[0:1, cols]).astype(BF16)
    normed_copy = pltpu.make_async_copy(normed_b, normed_out, store_sem.at[1])
    normed_copy.start()

    pltpu.make_async_copy(part, part, power_sem.at[0]).wait()
    wait_send(h_send, 0)
    wait_send(z_send, 1)
    wait_send(y_send, 2)
    stream_copy.wait()
    normed_copy.wait()


def per_device(constants, q_proj, k_proj, v_proj, short_weight, long_filter, long_bias, residual, norm_gain):
    tokens, channels = q_proj.shape
    pieces, groups = lax.axis_size("seq"), lax.axis_size("ch")
    own = channels // pieces
    block = (tokens, channels)
    operands = (
        q_proj, k_proj, v_proj, long_filter, residual, short_weight,
        long_bias.reshape(1, channels), norm_gain.reshape(1, channels),
    ) + constants
    scratch = [pltpu.VMEM(block, BF16) for _ in range(5)]
    scratch += [pltpu.VMEM(x.shape, x.dtype) for x in operands[5:]]
    scratch += [pltpu.VMEM((tokens + 8, channels), F32) for _ in range(3)]
    scratch += [pltpu.VMEM((8, channels), F32) for _ in range(2)]
    scratch += [pltpu.VMEM((channels, tokens), BF16) for _ in range(6)]
    scratch += [pltpu.VMEM((channels, tokens), F32) for _ in range(3)]
    scratch += [
        pltpu.VMEM((tokens // LANES, channels, LANES), F32),
        pltpu.VMEM((own * LANES, 2 * LANES), F32),
        pltpu.VMEM((tokens // LANES, channels, LANES), F32),
        pltpu.VMEM((groups, 1, tokens), F32),
        pltpu.VMEM(block, BF16),
        pltpu.VMEM(block, BF16),
    ]
    scratch += [pltpu.SemaphoreType.DMA((count,)) for count in (14, 2, 3, 3, 2, 2)]
    anywhere = pl.BlockSpec(memory_space=pl.ANY)
    return pl.pallas_call(
        functools.partial(kernel, pieces, groups),
        out_shape=(jax.ShapeDtypeStruct(block, BF16),) * 2,
        in_specs=[anywhere] * len(operands),
        out_specs=(anywhere,) * 2,
        scratch_shapes=scratch,
        compiler_params=pltpu.CompilerParams(
            collective_id=0, has_side_effects=True, vmem_limit_bytes=48 * 2**20
        ),
        cost_estimate=pl.CostEstimate(flops=1_300_000_000, bytes_accessed=4_000_000, transcendentals=0),
    )(*operands)


def solution(mesh):
    pieces = mesh.shape["seq"]
    constants = tuple(jnp.asarray(x) for x in tables(pieces))
    placed = (
        P("seq", "ch"),
        P("seq", "ch"),
        P("seq", "ch"),
        P(None, None, "ch"),
        P("seq", "ch"),
        P("ch"),
        P("seq", "ch"),
        P("ch"),
    )
    return jax.shard_map(
        functools.partial(per_device, constants),
        mesh=mesh,
        in_specs=placed,
        out_specs=(P("seq", "ch"), P("seq", "ch")),
        check_vma=False,
    )
```

```python
import functools
import math

import jax
import jax.numpy as jnp
import ml_dtypes
import numpy as np
from jax import lax
from jax.experimental import pallas as pl
from jax.experimental.pallas import tpu as pltpu
from jax.sharding import PartitionSpec as P

D = 4096
MESH = pl.DeviceIdType.MESH
F32 = jnp.float32
BF16 = jnp.bfloat16
LANES = 128


def tables(pieces):
    n = LANES
    quarter = np.arange(n) + 0.25
    per = n // pieces
    rows = np.array([per * (r % pieces) + r // pieces for r in range(n)])
    angle = 2 * math.pi / n * (quarter[:, None] * rows[None, :] % n)
    first = np.concatenate([np.cos(angle), -np.sin(angle)], axis=0)
    last = np.concatenate([np.cos(angle.T), -np.sin(angle.T)], axis=1) / (n * n)
    points = np.arange(n)
    angle = 2 * math.pi / n * (points[:, None] * points[None, :] % n)
    cosine, sine = np.cos(angle), np.sin(angle)
    second = np.block([[cosine, -sine], [sine, cosine]])
    angle = 2 * math.pi / (n * n) * (quarter[:, None] * points[None, :])
    return (
        first.astype(ml_dtypes.bfloat16),
        second.astype(ml_dtypes.bfloat16),
        second.T.copy().astype(ml_dtypes.bfloat16),
        last.astype(ml_dtypes.bfloat16),
        np.cos(angle).astype(np.float32),
        np.sin(angle).astype(np.float32),
    )


def dot(left, right):
    return jnp.dot(left, right, preferred_element_type=F32)


def order(step, count):
    half = (step + 1) // 2
    return lax.rem(count // 2 + jnp.where(lax.rem(step, 2) == 1, -half, half), count)


def kernel(
    pieces,
    groups,
    q_in, k_in, v_in, h_in, res_in, taps_in, bias_in, gain_in,
    first_in, second_in, third_in, last_in, cos_in, sin_in,
    stream_out, normed_out,
    q_b, k_b, v_b, h_b, res_b, taps, bias, gain,
    first, second, third, last, cos_t, sin_t,
    pad_q, pad_k, pad_v, halo_out, halo_in,
    h_send, h_recv, z_send, z_recv, y_send, y_recv, pregate_b,
    gate_t, skip_t, res_t, flat, spectrum_h, product, power_slots, normed_b, stream_b,
    load_sem, halo_sem, send_sem, recv_sem, power_sem, store_sem,
):
    me, ch = lax.axis_index("seq"), lax.axis_index("ch")
    tokens, channels = h_b.shape
    own = channels // pieces
    blocks = tokens // LANES
    wide = channels // LANES
    line = 4
    rings = pieces // line

    def peer(step):
        z = lax.rem(me // line + order(step // line, rings), rings)
        y = lax.rem(lax.rem(me, line) + order(lax.rem(step, line), line), line)
        return z * line + y

    barrier = pltpu.get_barrier_semaphore()

    def greet(step, _):
        pl.semaphore_signal(barrier, inc=1, device_id=(peer(step), ch), device_id_type=MESH)
        return 0

    lax.fori_loop(0, pieces - 1, greet, 0)

    def greet_row(d, _):
        pl.semaphore_signal(barrier, inc=1, device_id=(me, lax.rem(ch + d, groups)), device_id_type=MESH)
        return 0

    lax.fori_loop(1, groups, greet_row, 0)

    pairs = [
        (h_in, h_b), (q_in, q_b), (k_in, k_b), (v_in, v_b), (taps_in, taps), (bias_in, bias), (first_in, first),
        (second_in, second), (third_in, third), (last_in, last), (cos_in, cos_t), (sin_in, sin_t),
        (res_in, res_b), (gain_in, gain),
    ]
    loads = [pltpu.make_async_copy(src, dst, load_sem.at[i]) for i, (src, dst) in enumerate(pairs)]
    for load in loads:
        load.start()

    def tile(r, c):
        return slice(r * LANES, (r + 1) * LANES), slice(c * LANES, (c + 1) * LANES)

    loads[0].wait()
    for r in range(blocks):
        for c in range(wide):
            rows, cols = tile(r, c)
            h_send[cols, rows] = h_b[rows, cols].T

    for i in (1, 2, 3):
        loads[i].wait()
    tails = [x[tokens - 16 :, :].astype(F32)[14:, :] for x in (q_b, k_b, v_b)]
    halo_out[...] = jnp.concatenate(tails + [jnp.zeros((2, channels), F32)], axis=0)

    pl.semaphore_wait(barrier, pieces - 1 + groups - 1)

    halo_copy = pltpu.make_async_remote_copy(
        src_ref=halo_out, dst_ref=halo_in, send_sem=halo_sem.at[0], recv_sem=halo_sem.at[1],
        device_id=(lax.rem(me + 1, pieces), ch), device_id_type=MESH,
    )

    @pl.when(me < pieces - 1)
    def _():
        halo_copy.start()

    def send_all(source, target, slot):
        def send(step, _):
            other = peer(step)
            pltpu.make_async_remote_copy(
                src_ref=source.at[pl.ds(pl.multiple_of(other * own, own), own)],
                dst_ref=target.at[pl.ds(pl.multiple_of(me * own, own), own)],
                send_sem=send_sem.at[slot], recv_sem=recv_sem.at[slot],
                device_id=(other, ch), device_id_type=MESH,
            ).start()
            return 0

        lax.fori_loop(0, pieces - 1, send, 0)
        mine = pl.ds(pl.multiple_of(me * own, own), own)
        pltpu.make_async_copy(source.at[mine], target.at[mine], recv_sem.at[slot]).start()

    def wait_recv(target, slot):
        pltpu.make_async_copy(target, target, recv_sem.at[slot]).wait()

    def wait_send(source, slot):
        part = source.at[pl.ds(0, channels - own)]
        pltpu.make_async_copy(part, part, send_sem.at[slot]).wait()

    send_all(h_send, h_recv, 0)

    @pl.when(me == 0)
    def _():
        halo_in[...] = jnp.zeros_like(halo_in)

    for x, padded in ((k_b, pad_k), (v_b, pad_v), (q_b, pad_q)):
        padded[8:, :] = x[...].astype(F32)

    @pl.when(me > 0)
    def _():
        halo_copy.wait_recv()

    @pl.when(me < pieces - 1)
    def _():
        halo_copy.wait_send()

    for i, padded in enumerate((pad_q, pad_k, pad_v)):
        padded[6:8, :] = halo_in[2 * i : 2 * i + 2, :]

    for i in (4, 5):
        loads[i].wait()

    def short(s, padded, r, c):
        cols = tile(r, c)[1]
        total = taps[s, 0:1, cols] * padded[8 + r * LANES : 8 + (r + 1) * LANES, cols]
        total += taps[s, 1:2, cols] * padded[7 + r * LANES : 7 + (r + 1) * LANES, cols]
        return total + taps[s, 2:3, cols] * padded[6 + r * LANES : 6 + (r + 1) * LANES, cols]

    half = blocks // 2
    for r in range(half):
        for c in range(wide):
            parts = []
            for e in range(2):
                rows, cols = tile(r + e * half, c)
                pregate = (short(1, pad_k, r + e * half, c) * short(2, pad_v, r + e * half, c)).astype(BF16)
                pregate_b[rows, cols] = pregate
                parts.append(pregate.astype(F32).T.reshape(LANES // own, 2, own // 2, LANES))
            rows, cols = tile(r, c)
            for part in range(2):
                z_send[part, cols, rows] = (
                    jnp.stack([x[:, part] for x in parts], axis=1).reshape(LANES, LANES).astype(BF16)
                )

    for part in range(2):
        send_all(z_send.at[part], z_recv.at[part], 1 + part)

    loads[12].wait()
    for r in range(blocks):
        for c in range(wide):
            rows, cols = tile(r, c)
            gate_t[cols, rows] = short(0, pad_q, r, c).T
            skip_t[cols, rows] = (pregate_b[rows, cols].astype(F32) * bias[0:1, cols]).T
            res_t[cols, rows] = res_b[rows, cols].T.astype(F32)

    for i in (6, 7, 8, 9, 10, 11, 13):
        loads[i].wait()

    def forward(signal):
        partial = dot(first[...], jnp.concatenate(signal, axis=1).astype(BF16))
        turned = []
        for e in range(2):
            real = partial[:LANES, e * LANES : (e + 1) * LANES]
            imag = partial[LANES:, e * LANES : (e + 1) * LANES]
            cosine, sine = cos_t[...], sin_t[...]
            turned.append(
                jnp.concatenate([real * cosine + imag * sine, imag * cosine - real * sine], axis=1).astype(BF16)
            )
        return dot(jnp.concatenate(turned, axis=0), second[...])

    def widen(received, count):
        def step(r, _):
            rows = pl.ds(pl.multiple_of(r * 64, 64), 64)
            for i in range(count):
                flat[i, rows, :] = received[rows, i * LANES : (i + 1) * LANES].astype(F32)
            return 0

        lax.fori_loop(0, channels // 64, step, 0)

    wait_recv(h_recv, 0)
    widen(h_recv, blocks)

    def filter_step(p, _):
        signal = [
            jnp.concatenate([flat[i, pl.ds(2 * p + e, pieces, stride=own), :] for i in range(blocks)], axis=0)
            for e in range(2)
        ]
        spectrum_h[pl.ds(pl.multiple_of(p * 256, 256), 256), :] = forward(signal)
        return 0

    lax.fori_loop(0, own // 2, filter_step, 0)

    for part in range(2):
        wait_recv(z_recv.at[part], 1 + part)
        widen(z_recv.at[part], half)

        def signal_step(p, _):
            signal = [
                jnp.concatenate(
                    [
                        flat[i % half, pl.ds((i // half) * (own // 2) + 2 * p + e, pieces, stride=own), :]
                        for i in range(blocks)
                    ],
                    axis=0,
                )
                for e in range(2)
            ]
            x = forward(signal)
            w = spectrum_h[pl.ds(pl.multiple_of((part * own // 4 + p) * 256, 256), 256), :]
            xr, xi, wr, wi = x[:, :LANES], x[:, LANES:], w[:, :LANES], w[:, LANES:]
            both = jnp.concatenate([xr * wr - xi * wi, xr * wi + xi * wr], axis=1).astype(BF16)
            back = dot(both, third[...])
            turned = []
            for e in range(2):
                real = back[e * LANES : (e + 1) * LANES, :LANES]
                imag = back[e * LANES : (e + 1) * LANES, LANES:]
                cosine, sine = cos_t[...], sin_t[...]
                turned.append(
                    jnp.concatenate([real * cosine - imag * sine, real * sine + imag * cosine], axis=0).astype(BF16)
                )
            result = dot(last[...], jnp.concatenate(turned, axis=1))
            for e in range(2):
                for i in range(blocks):
                    product[i % half, pl.ds((i // half) * (own // 2) + 2 * p + e, pieces, stride=own), :] = result[
                        i * pieces : (i + 1) * pieces, e * LANES : (e + 1) * LANES
                    ]
            return 0

        lax.fori_loop(0, own // 4, signal_step, 0, unroll=2)

        def narrow(r, _):
            rows = pl.ds(pl.multiple_of(r * 64, 64), 64)
            for i in range(half):
                y_send[part, rows, i * LANES : (i + 1) * LANES] = product[i, rows, :].astype(BF16)
            return 0

        lax.fori_loop(0, channels // 64, narrow, 0)
        send_all(y_send.at[part], y_recv.at[part], 3 + part)

    total = jnp.zeros((8, tokens), F32)
    for part in range(2):
        wait_recv(y_recv.at[part], 3 + part)

        def gate_step(j, total):
            conv = y_recv[part, pl.ds(pl.multiple_of(j * own, own), own), :].astype(F32)
            conv = jnp.concatenate([conv[: own // 2], conv[own // 2 :]], axis=1)
            rows = pl.ds(pl.multiple_of(j * own + part * (own // 2), 8), own // 2)
            mixed = (gate_t[rows, :] * (conv + skip_t[rows, :])).astype(BF16)
            stream = (res_t[rows, :] + mixed.astype(F32)).astype(BF16).astype(F32)
            res_t[rows, :] = stream
            return total + stream * stream

        total = lax.fori_loop(0, pieces, gate_step, total, unroll=4)
    power_slots[ch] = jnp.sum(total, axis=0, keepdims=True)

    def power_copy(d):
        other = lax.rem(ch + d, groups)
        return pltpu.make_async_remote_copy(
            src_ref=power_slots.at[ch], dst_ref=power_slots.at[ch],
            send_sem=power_sem.at[0], recv_sem=power_sem.at[1],
            device_id=(me, other), device_id_type=MESH,
        )

    for d in range(1, groups):
        power_copy(d).start()

    for r in range(blocks):
        for c in range(wide):
            rows, cols = tile(r, c)
            stream_b[rows, cols] = res_t[cols, rows].T.astype(BF16)
    stream_copy = pltpu.make_async_copy(stream_b, stream_out, store_sem.at[0])
    stream_copy.start()

    part = power_slots.at[pl.ds(0, groups - 1)]
    pltpu.make_async_copy(part, part, power_sem.at[1]).wait()
    power = jnp.sum(power_slots[...], axis=0) / D
    scale = lax.rsqrt(power + 1e-6)
    for r in range(blocks):
        rows = tile(r, 0)[0]
        column = jnp.broadcast_to(scale[:, rows], (LANES, LANES)).T
        for c in range(wide):
            cols = tile(r, c)[1]
            normed_b[rows, cols] = (stream_b[rows, cols].astype(F32) * column * gain[0:1, cols]).astype(BF16)
    normed_copy = pltpu.make_async_copy(normed_b, normed_out, store_sem.at[1])
    normed_copy.start()

    pltpu.make_async_copy(part, part, power_sem.at[0]).wait()
    wait_send(h_send, 0)
    for part in range(2):
        wait_send(z_send.at[part], 1 + part)
        wait_send(y_send.at[part], 3 + part)
    stream_copy.wait()
    normed_copy.wait()


def per_device(constants, q_proj, k_proj, v_proj, short_weight, long_filter, long_bias, residual, norm_gain):
    tokens, channels = q_proj.shape
    pieces, groups = lax.axis_size("seq"), lax.axis_size("ch")
    own = channels // pieces
    block = (tokens, channels)
    operands = (
        q_proj, k_proj, v_proj, long_filter, residual, short_weight,
        long_bias.reshape(1, channels), norm_gain.reshape(1, channels),
    ) + constants
    scratch = [pltpu.VMEM(block, BF16) for _ in range(5)]
    scratch += [pltpu.VMEM(x.shape, x.dtype) for x in operands[5:]]
    scratch += [pltpu.VMEM((tokens + 8, channels), F32) for _ in range(3)]
    scratch += [pltpu.VMEM((8, channels), F32) for _ in range(2)]
    scratch += [pltpu.VMEM((channels, tokens), BF16) for _ in range(2)]
    scratch += [pltpu.VMEM((2, channels, tokens // 2), BF16) for _ in range(4)]
    scratch += [pltpu.VMEM(block, BF16)]
    scratch += [pltpu.VMEM((channels, tokens), F32) for _ in range(3)]
    scratch += [
        pltpu.VMEM((tokens // LANES, channels, LANES), F32),
        pltpu.VMEM((own * LANES, 2 * LANES), F32),
        pltpu.VMEM((tokens // LANES // 2, channels, LANES), F32),
        pltpu.VMEM((groups, 1, tokens), F32),
        pltpu.VMEM(block, BF16),
        pltpu.VMEM(block, BF16),
    ]
    scratch += [pltpu.SemaphoreType.DMA((count,)) for count in (14, 2, 5, 5, 2, 2)]
    anywhere = pl.BlockSpec(memory_space=pl.ANY)
    return pl.pallas_call(
        functools.partial(kernel, pieces, groups),
        out_shape=(jax.ShapeDtypeStruct(block, BF16),) * 2,
        in_specs=[anywhere] * len(operands),
        out_specs=(anywhere,) * 2,
        scratch_shapes=scratch,
        compiler_params=pltpu.CompilerParams(
            collective_id=0, has_side_effects=True, vmem_limit_bytes=62 * 2**20
        ),
        cost_estimate=pl.CostEstimate(flops=1_300_000_000, bytes_accessed=4_000_000, transcendentals=0),
    )(*operands)


def solution(mesh):
    pieces = mesh.shape["seq"]
    constants = tuple(jnp.asarray(x) for x in tables(pieces))
    placed = (
        P("seq", "ch"),
        P("seq", "ch"),
        P("seq", "ch"),
        P(None, None, "ch"),
        P("seq", "ch"),
        P("ch"),
        P("seq", "ch"),
        P("ch"),
    )
    return jax.shard_map(
        functools.partial(per_device, constants),
        mesh=mesh,
        in_specs=placed,
        out_specs=(P("seq", "ch"), P("seq", "ch")),
        check_vma=False,
    )
```

```python
import functools
import math

import jax
import jax.numpy as jnp
import ml_dtypes
import numpy as np
from jax import lax
from jax.experimental import pallas as pl
from jax.experimental.pallas import tpu as pltpu
from jax.sharding import PartitionSpec as P

D = 4096
MESH = pl.DeviceIdType.MESH
F32 = jnp.float32
BF16 = jnp.bfloat16
LANES = 128


def tables(pieces):
    n = LANES
    quarter = np.arange(n) + 0.25
    per = n // pieces
    rows = np.array([per * (r % pieces) + r // pieces for r in range(n)])
    angle = 2 * math.pi / n * (quarter[:, None] * rows[None, :] % n)
    first = np.concatenate([np.cos(angle), -np.sin(angle)], axis=0)
    last = np.concatenate([np.cos(angle.T), -np.sin(angle.T)], axis=1) / (n * n)
    points = np.arange(n)
    angle = 2 * math.pi / n * (points[:, None] * points[None, :] % n)
    cosine, sine = np.cos(angle), np.sin(angle)
    second = np.block([[cosine, -sine], [sine, cosine]])
    angle = 2 * math.pi / (n * n) * (quarter[:, None] * points[None, :])
    return (
        first.astype(ml_dtypes.bfloat16),
        second.astype(ml_dtypes.bfloat16),
        second.T.copy().astype(ml_dtypes.bfloat16),
        last.astype(ml_dtypes.bfloat16),
        np.cos(angle).astype(np.float32),
        np.sin(angle).astype(np.float32),
    )


def dot(left, right):
    return jnp.dot(left, right, preferred_element_type=F32)


def order(step, count):
    half = (step + 1) // 2
    return lax.rem(count // 2 + jnp.where(lax.rem(step, 2) == 1, -half, half), count)


def kernel(
    pieces,
    groups,
    q_in, k_in, v_in, h_in, res_in, taps_in, bias_in, gain_in,
    first_in, second_in, third_in, last_in, cos_in, sin_in,
    stream_b, normed_b,
    q_b, k_b, v_b, h_b, res_b, taps, bias, gain,
    first, second, third, last, cos_t, sin_t,
    pad_q, pad_k, pad_v, halo_out, halo_in,
    h_send, h_recv, z_send, z_recv, y_send, y_recv, pregate_b,
    gate_t, skip_t, res_t, flat, spectrum_h, product, power_slots,
    load_sem, halo_sem, send_sem, recv_sem, power_sem,
):
    me, ch = lax.axis_index("seq"), lax.axis_index("ch")
    tokens, channels = h_b.shape
    own = channels // pieces
    blocks = tokens // LANES
    wide = channels // LANES
    line = 4
    rings = pieces // line

    def peer(step):
        z = lax.rem(me // line + order(step // line, rings), rings)
        y = lax.rem(lax.rem(me, line) + order(lax.rem(step, line), line), line)
        return z * line + y

    def early(step):
        z = lax.rem(step // line, 2) * (rings // 2) + step // (2 * line)
        y = lax.rem(lax.rem(me, line) + order(lax.rem(step, line), line), line)
        return z * line + y

    pairs = [
        (h_in, h_b), (q_in, q_b), (k_in, k_b), (v_in, v_b), (taps_in, taps), (bias_in, bias), (first_in, first),
        (second_in, second), (third_in, third), (last_in, last), (cos_in, cos_t), (sin_in, sin_t),
        (res_in, res_b), (gain_in, gain),
    ]
    loads = [pltpu.make_async_copy(src, dst, load_sem.at[i]) for i, (src, dst) in enumerate(pairs)]
    for load in loads[:4]:
        load.start()

    barrier = pltpu.get_barrier_semaphore()

    def greet(step, _):
        pl.semaphore_signal(barrier, inc=1, device_id=(peer(step), ch), device_id_type=MESH)
        return 0

    lax.fori_loop(0, pieces - 1, greet, 0)

    def greet_row(d, _):
        pl.semaphore_signal(barrier, inc=1, device_id=(me, lax.rem(ch + d, groups)), device_id_type=MESH)
        return 0

    lax.fori_loop(1, groups, greet_row, 0)

    def tile(r, c):
        return slice(r * LANES, (r + 1) * LANES), slice(c * LANES, (c + 1) * LANES)

    for load in loads[4:]:
        load.start()

    loads[0].wait()
    for r in range(blocks):
        for c in range(wide):
            rows, cols = tile(r, c)
            h_send[cols, rows] = h_b[rows, cols].T

    for i in (1, 2, 3):
        loads[i].wait()
    tails = [x[tokens - 16 :, :].astype(F32)[14:, :] for x in (q_b, k_b, v_b)]
    halo_out[...] = jnp.concatenate(tails + [jnp.zeros((2, channels), F32)], axis=0)

    pl.semaphore_wait(barrier, pieces - 1 + groups - 1)

    halo_copy = pltpu.make_async_remote_copy(
        src_ref=halo_out, dst_ref=halo_in, send_sem=halo_sem.at[0], recv_sem=halo_sem.at[1],
        device_id=(lax.rem(me + 1, pieces), ch), device_id_type=MESH,
    )

    @pl.when(me < pieces - 1)
    def _():
        halo_copy.start()

    def send_all(source, target, slot, partner=peer):
        def send(step, _):
            other = partner(step)

            @pl.when(other != me)
            def _():
                pltpu.make_async_remote_copy(
                    src_ref=source.at[pl.ds(pl.multiple_of(other * own, own), own)],
                    dst_ref=target.at[pl.ds(pl.multiple_of(me * own, own), own)],
                    send_sem=send_sem.at[slot], recv_sem=recv_sem.at[slot],
                    device_id=(other, ch), device_id_type=MESH,
                ).start()

            return 0

        lax.fori_loop(0, pieces, send, 0)
        mine = pl.ds(pl.multiple_of(me * own, own), own)
        pltpu.make_async_copy(source.at[mine], target.at[mine], recv_sem.at[slot]).start()

    def wait_recv(target, slot):
        pltpu.make_async_copy(target, target, recv_sem.at[slot]).wait()

    def wait_send(source, slot):
        part = source.at[pl.ds(0, channels - own)]
        pltpu.make_async_copy(part, part, send_sem.at[slot]).wait()

    send_all(h_send, h_recv, 0)

    @pl.when(me == 0)
    def _():
        halo_in[...] = jnp.zeros_like(halo_in)

    for x, padded in ((k_b, pad_k), (v_b, pad_v), (q_b, pad_q)):
        padded[8:, :] = x[...].astype(F32)

    @pl.when(me > 0)
    def _():
        halo_copy.wait_recv()

    @pl.when(me < pieces - 1)
    def _():
        halo_copy.wait_send()

    for i, padded in enumerate((pad_q, pad_k, pad_v)):
        padded[6:8, :] = halo_in[2 * i : 2 * i + 2, :]

    for i in (4, 5):
        loads[i].wait()

    def short(s, padded, r, c):
        cols = tile(r, c)[1]
        total = taps[s, 0:1, cols] * padded[8 + r * LANES : 8 + (r + 1) * LANES, cols]
        total += taps[s, 1:2, cols] * padded[7 + r * LANES : 7 + (r + 1) * LANES, cols]
        return total + taps[s, 2:3, cols] * padded[6 + r * LANES : 6 + (r + 1) * LANES, cols]

    half = blocks // 2
    for r in range(half):
        for c in range(wide):
            parts = []
            for e in range(2):
                rows, cols = tile(r + e * half, c)
                pregate = (short(1, pad_k, r + e * half, c) * short(2, pad_v, r + e * half, c)).astype(BF16)
                pregate_b[rows, cols] = pregate
                parts.append(pregate.astype(F32).T.reshape(LANES // own, 2, own // 2, LANES))
            rows, cols = tile(r, c)
            for part in range(2):
                z_send[part, cols, rows] = (
                    jnp.stack([x[:, part] for x in parts], axis=1).reshape(LANES, LANES).astype(BF16)
                )

    for part in range(2):
        send_all(z_send.at[part], z_recv.at[part], 1 + part)

    loads[12].wait()
    for r in range(blocks):
        for c in range(wide):
            rows, cols = tile(r, c)
            gate_t[cols, rows] = short(0, pad_q, r, c).T
            skip_t[cols, rows] = (pregate_b[rows, cols].astype(F32) * bias[0:1, cols]).T
            res_t[cols, rows] = res_b[rows, cols].T.astype(F32)

    for i in (6, 7, 8, 9, 10, 11, 13):
        loads[i].wait()

    def forward(signal):
        partial = dot(first[...], jnp.concatenate(signal, axis=1).astype(BF16))
        turned = []
        for e in range(2):
            real = partial[:LANES, e * LANES : (e + 1) * LANES]
            imag = partial[LANES:, e * LANES : (e + 1) * LANES]
            cosine, sine = cos_t[...], sin_t[...]
            turned.append(
                jnp.concatenate([real * cosine + imag * sine, imag * cosine - real * sine], axis=1).astype(BF16)
            )
        return dot(jnp.concatenate(turned, axis=0), second[...])

    def widen(received, count):
        def step(r, _):
            rows = pl.ds(pl.multiple_of(r * 64, 64), 64)
            for i in range(count):
                flat[i, rows, :] = received[rows, i * LANES : (i + 1) * LANES].astype(F32)
            return 0

        lax.fori_loop(0, channels // 64, step, 0)

    wait_recv(h_recv, 0)
    widen(h_recv, blocks)

    def filter_step(p, _):
        signal = [
            jnp.concatenate([flat[i, pl.ds(2 * p + e, pieces, stride=own), :] for i in range(blocks)], axis=0)
            for e in range(2)
        ]
        spectrum_h[pl.ds(pl.multiple_of(p * 256, 256), 256), :] = forward(signal)
        return 0

    lax.fori_loop(0, own // 2, filter_step, 0)

    for part in range(2):
        wait_recv(z_recv.at[part], 1 + part)
        widen(z_recv.at[part], half)

        def signal_step(p, _):
            signal = [
                jnp.concatenate(
                    [
                        flat[i % half, pl.ds((i // half) * (own // 2) + 2 * p + e, pieces, stride=own), :]
                        for i in range(blocks)
                    ],
                    axis=0,
                )
                for e in range(2)
            ]
            x = forward(signal)
            w = spectrum_h[pl.ds(pl.multiple_of((part * own // 4 + p) * 256, 256), 256), :]
            xr, xi, wr, wi = x[:, :LANES], x[:, LANES:], w[:, :LANES], w[:, LANES:]
            both = jnp.concatenate([xr * wr - xi * wi, xr * wi + xi * wr], axis=1).astype(BF16)
            back = dot(both, third[...])
            turned = []
            for e in range(2):
                real = back[e * LANES : (e + 1) * LANES, :LANES]
                imag = back[e * LANES : (e + 1) * LANES, LANES:]
                cosine, sine = cos_t[...], sin_t[...]
                turned.append(
                    jnp.concatenate([real * cosine - imag * sine, real * sine + imag * cosine], axis=0).astype(BF16)
                )
            result = dot(last[...], jnp.concatenate(turned, axis=1))
            for e in range(2):
                for i in range(blocks):
                    product[i % half, pl.ds((i // half) * (own // 2) + 2 * p + e, pieces, stride=own), :] = result[
                        i * pieces : (i + 1) * pieces, e * LANES : (e + 1) * LANES
                    ]
            return 0

        lax.fori_loop(0, own // 4, signal_step, 0, unroll=2)

        def narrow(r, _):
            rows = pl.ds(pl.multiple_of(r * 64, 64), 64)
            for i in range(half):
                y_send[part, rows, i * LANES : (i + 1) * LANES] = product[i, rows, :].astype(BF16)
            return 0

        lax.fori_loop(0, channels // 64, narrow, 0)
        send_all(y_send.at[part], y_recv.at[part], 3 + part, early if part else peer)

    total = jnp.zeros((8, tokens), F32)
    for part in range(2):
        wait_recv(y_recv.at[part], 3 + part)

        def gate_step(j, total):
            conv = y_recv[part, pl.ds(pl.multiple_of(j * own, own), own), :].astype(F32)
            conv = jnp.concatenate([conv[: own // 2], conv[own // 2 :]], axis=1)
            rows = pl.ds(pl.multiple_of(j * own + part * (own // 2), 8), own // 2)
            mixed = (gate_t[rows, :] * (conv + skip_t[rows, :])).astype(BF16)
            stream = (res_t[rows, :] + mixed.astype(F32)).astype(BF16).astype(F32)
            res_t[rows, :] = stream
            return total + stream * stream

        total = lax.fori_loop(0, pieces, gate_step, total, unroll=4)
    power_slots[ch] = jnp.sum(total, axis=0, keepdims=True)

    def power_copy(d):
        other = lax.rem(ch + d, groups)
        return pltpu.make_async_remote_copy(
            src_ref=power_slots.at[ch], dst_ref=power_slots.at[ch],
            send_sem=power_sem.at[0], recv_sem=power_sem.at[1],
            device_id=(me, other), device_id_type=MESH,
        )

    for d in range(1, groups):
        power_copy(d).start()

    for r in range(blocks):
        for c in range(wide):
            rows, cols = tile(r, c)
            stream_b[rows, cols] = res_t[cols, rows].T.astype(BF16)

    part = power_slots.at[pl.ds(0, groups - 1)]
    pltpu.make_async_copy(part, part, power_sem.at[1]).wait()
    power = jnp.sum(power_slots[...], axis=0) / D
    scale = lax.rsqrt(power + 1e-6)
    for r in range(blocks):
        rows = tile(r, 0)[0]
        column = jnp.broadcast_to(scale[:, rows], (LANES, LANES)).T
        for c in range(wide):
            cols = tile(r, c)[1]
            normed_b[rows, cols] = (stream_b[rows, cols].astype(F32) * column * gain[0:1, cols]).astype(BF16)

    pltpu.make_async_copy(part, part, power_sem.at[0]).wait()
    wait_send(h_send, 0)
    for part in range(2):
        wait_send(z_send.at[part], 1 + part)
        wait_send(y_send.at[part], 3 + part)


def per_device(constants, q_proj, k_proj, v_proj, short_weight, long_filter, long_bias, residual, norm_gain):
    tokens, channels = q_proj.shape
    pieces, groups = lax.axis_size("seq"), lax.axis_size("ch")
    own = channels // pieces
    block = (tokens, channels)
    operands = (
        q_proj, k_proj, v_proj, long_filter, residual, short_weight,
        long_bias.reshape(1, channels), norm_gain.reshape(1, channels),
    ) + constants
    scratch = [pltpu.VMEM(block, BF16) for _ in range(5)]
    scratch += [pltpu.VMEM(x.shape, x.dtype) for x in operands[5:]]
    scratch += [pltpu.VMEM((tokens + 8, channels), F32) for _ in range(3)]
    scratch += [pltpu.VMEM((8, channels), F32) for _ in range(2)]
    scratch += [pltpu.VMEM((channels, tokens), BF16) for _ in range(2)]
    scratch += [pltpu.VMEM((2, channels, tokens // 2), BF16) for _ in range(4)]
    scratch += [pltpu.VMEM(block, BF16)]
    scratch += [pltpu.VMEM((channels, tokens), F32) for _ in range(3)]
    scratch += [
        pltpu.VMEM((tokens // LANES, channels, LANES), F32),
        pltpu.VMEM((own * LANES, 2 * LANES), F32),
        pltpu.VMEM((tokens // LANES // 2, channels, LANES), F32),
        pltpu.VMEM((groups, 1, tokens), F32),
    ]
    scratch += [pltpu.SemaphoreType.DMA((count,)) for count in (14, 2, 5, 5, 2)]
    anywhere = pl.BlockSpec(memory_space=pl.ANY)
    operands = tuple(pltpu.with_memory_space_constraint(x, pltpu.HBM) for x in operands)
    return pl.pallas_call(
        functools.partial(kernel, pieces, groups),
        out_shape=(jax.ShapeDtypeStruct(block, BF16),) * 2,
        in_specs=[anywhere] * len(operands),
        out_specs=(pl.BlockSpec(memory_space=pltpu.VMEM),) * 2,
        scratch_shapes=scratch,
        compiler_params=pltpu.CompilerParams(
            collective_id=0, has_side_effects=True, vmem_limit_bytes=32 * 2**20
        ),
        cost_estimate=pl.CostEstimate(flops=1_300_000_000, bytes_accessed=4_000_000, transcendentals=0),
    )(*operands)


def solution(mesh):
    pieces = mesh.shape["seq"]
    constants = tuple(jnp.asarray(x) for x in tables(pieces))
    placed = (
        P("seq", "ch"),
        P("seq", "ch"),
        P("seq", "ch"),
        P(None, None, "ch"),
        P("seq", "ch"),
        P("ch"),
        P("seq", "ch"),
        P("ch"),
    )
    return jax.shard_map(
        functools.partial(per_device, constants),
        mesh=mesh,
        in_specs=placed,
        out_specs=(P("seq", "ch"), P("seq", "ch")),
        check_vma=False,
    )
```

```python
import functools
import math

import jax
import jax.numpy as jnp
import ml_dtypes
import numpy as np
from jax import lax
from jax.experimental import pallas as pl
from jax.experimental.pallas import tpu as pltpu
from jax.sharding import PartitionSpec as P

D = 4096
MESH = pl.DeviceIdType.MESH
F32 = jnp.float32
BF16 = jnp.bfloat16
LANES = 128


def tables(pieces):
    n = LANES
    quarter = np.arange(n) + 0.25
    per = n // pieces
    rows = np.array([per * (r % pieces) + r // pieces for r in range(n)])
    angle = 2 * math.pi / n * (quarter[:, None] * rows[None, :] % n)
    first = np.concatenate([np.cos(angle), -np.sin(angle)], axis=0)
    last = np.concatenate([np.cos(angle.T), -np.sin(angle.T)], axis=1) / (n * n)
    points = np.arange(n)
    angle = 2 * math.pi / n * (points[:, None] * points[None, :] % n)
    cosine, sine = np.cos(angle), np.sin(angle)
    second = np.block([[cosine, -sine], [sine, cosine]])
    angle = 2 * math.pi / (n * n) * (quarter[:, None] * points[None, :])
    return (
        first.astype(ml_dtypes.bfloat16),
        second.astype(ml_dtypes.bfloat16),
        second.T.copy().astype(ml_dtypes.bfloat16),
        last.astype(ml_dtypes.bfloat16),
        np.cos(angle).astype(np.float32),
        np.sin(angle).astype(np.float32),
    )


def dot(left, right):
    return jnp.dot(left, right, preferred_element_type=F32)


def order(step, count):
    half = (step + 1) // 2
    return lax.rem(count // 2 + jnp.where(lax.rem(step, 2) == 1, -half, half), count)


def kernel(
    pieces,
    groups,
    q_in, k_in, v_in, h_in, res_in, taps_in, bias_in, gain_in,
    first_in, second_in, third_in, last_in, cos_in, sin_in,
    both,
    q_b, k_b, v_b, h_b, res_b, taps, bias, gain,
    first, second, third, last, cos_t, sin_t,
    pad_q, pad_k, pad_v, halo_out, halo_in,
    h_send, h_recv, z_send, z_recv, y_send, y_recv, pregate_b,
    gate_t, skip_t, res_t, flat, spectrum_h, product, power_slots,
    load_sem, halo_sem, send_sem, recv_sem, power_sem,
):
    me, ch = lax.axis_index("seq"), lax.axis_index("ch")
    tokens, channels = h_b.shape
    own = channels // pieces
    blocks = tokens // LANES
    wide = channels // LANES
    line = 4
    rings = pieces // line

    def peer(step):
        z = lax.rem(me // line + order(step // line, rings), rings)
        y = lax.rem(lax.rem(me, line) + order(lax.rem(step, line), line), line)
        return z * line + y

    def early(step):
        z = lax.rem(step // line, 2) * (rings // 2) + step // (2 * line)
        y = lax.rem(lax.rem(me, line) + order(lax.rem(step, line), line), line)
        return z * line + y

    pairs = [
        (h_in, h_b), (q_in, q_b), (k_in, k_b), (v_in, v_b), (taps_in, taps), (bias_in, bias), (first_in, first),
        (second_in, second), (third_in, third), (last_in, last), (cos_in, cos_t), (sin_in, sin_t),
        (res_in, res_b), (gain_in, gain),
    ]
    loads = [pltpu.make_async_copy(src, dst, load_sem.at[i]) for i, (src, dst) in enumerate(pairs)]
    for load in loads[:4]:
        load.start()

    barrier = pltpu.get_barrier_semaphore()

    def greet(step, _):
        pl.semaphore_signal(barrier, inc=1, device_id=(peer(step), ch), device_id_type=MESH)
        return 0

    lax.fori_loop(0, pieces - 1, greet, 0)

    def greet_row(d, _):
        pl.semaphore_signal(barrier, inc=1, device_id=(me, lax.rem(ch + d, groups)), device_id_type=MESH)
        return 0

    lax.fori_loop(1, groups, greet_row, 0)

    def tile(r, c):
        return slice(r * LANES, (r + 1) * LANES), slice(c * LANES, (c + 1) * LANES)

    for load in loads[4:]:
        load.start()

    loads[0].wait()
    for r in range(blocks):
        for c in range(wide):
            rows, cols = tile(r, c)
            h_send[cols, rows] = h_b[rows, cols].T

    for i in (1, 2, 3):
        loads[i].wait()
    tails = [x[tokens - 16 :, :].astype(F32)[14:, :] for x in (q_b, k_b, v_b)]
    halo_out[...] = jnp.concatenate(tails + [jnp.zeros((2, channels), F32)], axis=0)

    pl.semaphore_wait(barrier, pieces - 1 + groups - 1)

    halo_copy = pltpu.make_async_remote_copy(
        src_ref=halo_out, dst_ref=halo_in, send_sem=halo_sem.at[0], recv_sem=halo_sem.at[1],
        device_id=(lax.rem(me + 1, pieces), ch), device_id_type=MESH,
    )

    @pl.when(me < pieces - 1)
    def _():
        halo_copy.start()

    def send_all(source, target, slot, partner=peer):
        def send(step, _):
            other = partner(step)

            @pl.when(other != me)
            def _():
                pltpu.make_async_remote_copy(
                    src_ref=source.at[pl.ds(pl.multiple_of(other * own, own), own)],
                    dst_ref=target.at[pl.ds(pl.multiple_of(me * own, own), own)],
                    send_sem=send_sem.at[slot], recv_sem=recv_sem.at[slot],
                    device_id=(other, ch), device_id_type=MESH,
                ).start()

            return 0

        lax.fori_loop(0, pieces, send, 0)
        mine = pl.ds(pl.multiple_of(me * own, own), own)
        pltpu.make_async_copy(source.at[mine], target.at[mine], recv_sem.at[slot]).start()

    def wait_recv(target, slot):
        pltpu.make_async_copy(target, target, recv_sem.at[slot]).wait()

    def wait_send(source, slot):
        part = source.at[pl.ds(0, channels - own)]
        pltpu.make_async_copy(part, part, send_sem.at[slot]).wait()

    send_all(h_send, h_recv, 0)

    @pl.when(me == 0)
    def _():
        halo_in[...] = jnp.zeros_like(halo_in)

    for x, padded in ((k_b, pad_k), (v_b, pad_v), (q_b, pad_q)):
        padded[8:, :] = x[...].astype(F32)

    @pl.when(me > 0)
    def _():
        halo_copy.wait_recv()

    @pl.when(me < pieces - 1)
    def _():
        halo_copy.wait_send()

    for i, padded in enumerate((pad_q, pad_k, pad_v)):
        padded[6:8, :] = halo_in[2 * i : 2 * i + 2, :]

    for i in (4, 5):
        loads[i].wait()

    def short(s, padded, r, c):
        cols = tile(r, c)[1]
        total = taps[s, 0:1, cols] * padded[8 + r * LANES : 8 + (r + 1) * LANES, cols]
        total += taps[s, 1:2, cols] * padded[7 + r * LANES : 7 + (r + 1) * LANES, cols]
        return total + taps[s, 2:3, cols] * padded[6 + r * LANES : 6 + (r + 1) * LANES, cols]

    half = blocks // 2
    for r in range(half):
        for c in range(wide):
            parts = []
            for e in range(2):
                rows, cols = tile(r + e * half, c)
                pregate = (short(1, pad_k, r + e * half, c) * short(2, pad_v, r + e * half, c)).astype(BF16)
                pregate_b[rows, cols] = pregate
                parts.append(pregate.astype(F32).T.reshape(LANES // own, 2, own // 2, LANES))
            rows, cols = tile(r, c)
            for part in range(2):
                z_send[part, cols, rows] = (
                    jnp.stack([x[:, part] for x in parts], axis=1).reshape(LANES, LANES).astype(BF16)
                )

    for part in range(2):
        send_all(z_send.at[part], z_recv.at[part], 1 + part)

    loads[12].wait()
    for r in range(blocks):
        for c in range(wide):
            rows, cols = tile(r, c)
            gate_t[cols, rows] = short(0, pad_q, r, c).T
            skip_t[cols, rows] = (pregate_b[rows, cols].astype(F32) * bias[0:1, cols]).T
            res_t[cols, rows] = res_b[rows, cols].T.astype(F32)

    for i in (6, 7, 8, 9, 10, 11, 13):
        loads[i].wait()

    def forward(signal):
        partial = dot(first[...], jnp.concatenate(signal, axis=1).astype(BF16))
        turned = []
        for e in range(2):
            real = partial[:LANES, e * LANES : (e + 1) * LANES]
            imag = partial[LANES:, e * LANES : (e + 1) * LANES]
            cosine, sine = cos_t[...], sin_t[...]
            turned.append(
                jnp.concatenate([real * cosine + imag * sine, imag * cosine - real * sine], axis=1).astype(BF16)
            )
        return dot(jnp.concatenate(turned, axis=0), second[...])

    def widen(received, count):
        def step(r, _):
            rows = pl.ds(pl.multiple_of(r * 64, 64), 64)
            for i in range(count):
                flat[i, rows, :] = received[rows, i * LANES : (i + 1) * LANES].astype(F32)
            return 0

        lax.fori_loop(0, channels // 64, step, 0, unroll=4)

    wait_recv(h_recv, 0)
    widen(h_recv, blocks)

    def filter_step(p, _):
        signal = [
            jnp.concatenate([flat[i, pl.ds(2 * p + e, pieces, stride=own), :] for i in range(blocks)], axis=0)
            for e in range(2)
        ]
        spectrum_h[pl.ds(pl.multiple_of(p * 256, 256), 256), :] = forward(signal)
        return 0

    lax.fori_loop(0, own // 2, filter_step, 0, unroll=4)

    for part in range(2):
        wait_recv(z_recv.at[part], 1 + part)
        widen(z_recv.at[part], half)

        def signal_step(p, _):
            signal = [
                jnp.concatenate(
                    [
                        flat[i % half, pl.ds((i // half) * (own // 2) + 2 * p + e, pieces, stride=own), :]
                        for i in range(blocks)
                    ],
                    axis=0,
                )
                for e in range(2)
            ]
            x = forward(signal)
            w = spectrum_h[pl.ds(pl.multiple_of((part * own // 4 + p) * 256, 256), 256), :]
            xr, xi, wr, wi = x[:, :LANES], x[:, LANES:], w[:, :LANES], w[:, LANES:]
            both = jnp.concatenate([xr * wr - xi * wi, xr * wi + xi * wr], axis=1).astype(BF16)
            back = dot(both, third[...])
            turned = []
            for e in range(2):
                real = back[e * LANES : (e + 1) * LANES, :LANES]
                imag = back[e * LANES : (e + 1) * LANES, LANES:]
                cosine, sine = cos_t[...], sin_t[...]
                turned.append(
                    jnp.concatenate([real * cosine - imag * sine, real * sine + imag * cosine], axis=0).astype(BF16)
                )
            result = dot(last[...], jnp.concatenate(turned, axis=1))
            for e in range(2):
                for i in range(blocks):
                    product[i % half, pl.ds((i // half) * (own // 2) + 2 * p + e, pieces, stride=own), :] = result[
                        i * pieces : (i + 1) * pieces, e * LANES : (e + 1) * LANES
                    ]
            return 0

        lax.fori_loop(0, own // 4, signal_step, 0, unroll=4)

        def narrow(r, _):
            rows = pl.ds(pl.multiple_of(r * 64, 64), 64)
            for i in range(half):
                y_send[part, rows, i * LANES : (i + 1) * LANES] = product[i, rows, :].astype(BF16)
            return 0

        lax.fori_loop(0, channels // 64, narrow, 0, unroll=4)
        send_all(y_send.at[part], y_recv.at[part], 3 + part, early if part else peer)

    total = jnp.zeros((8, tokens), F32)
    for part in range(2):
        wait_recv(y_recv.at[part], 3 + part)

        def gate_step(j, total):
            conv = y_recv[part, pl.ds(pl.multiple_of(j * own, own), own), :].astype(F32)
            conv = jnp.concatenate([conv[: own // 2], conv[own // 2 :]], axis=1)
            rows = pl.ds(pl.multiple_of(j * own + part * (own // 2), 8), own // 2)
            mixed = (gate_t[rows, :] * (conv + skip_t[rows, :])).astype(BF16)
            stream = (res_t[rows, :] + mixed.astype(F32)).astype(BF16).astype(F32)
            res_t[rows, :] = stream
            return total + stream * stream

        total = lax.fori_loop(0, pieces, gate_step, total, unroll=8)
    power_slots[ch] = jnp.sum(total, axis=0, keepdims=True)

    def power_copy(d):
        other = lax.rem(ch + d, groups)
        return pltpu.make_async_remote_copy(
            src_ref=power_slots.at[ch], dst_ref=power_slots.at[ch],
            send_sem=power_sem.at[0], recv_sem=power_sem.at[1],
            device_id=(me, other), device_id_type=MESH,
        )

    for d in (4, 3, 5, 2, 6, 7, 1):
        power_copy(d).start()

    for r in range(blocks):
        for c in range(wide):
            rows, cols = tile(r, c)
            both[0, rows, cols] = res_t[cols, rows].T.astype(BF16)

    part = power_slots.at[pl.ds(0, groups - 1)]
    pltpu.make_async_copy(part, part, power_sem.at[1]).wait()
    power = jnp.sum(power_slots[...], axis=0) / D
    scale = lax.rsqrt(power + 1e-6)
    for r in range(blocks):
        rows = tile(r, 0)[0]
        column = jnp.broadcast_to(scale[:, rows], (LANES, LANES)).T
        for c in range(wide):
            cols = tile(r, c)[1]
            both[1, rows, cols] = (both[0, rows, cols].astype(F32) * column * gain[0:1, cols]).astype(BF16)

    pltpu.make_async_copy(part, part, power_sem.at[0]).wait()
    wait_send(h_send, 0)
    for part in range(2):
        wait_send(z_send.at[part], 1 + part)
        wait_send(y_send.at[part], 3 + part)


def per_device(constants, q_proj, k_proj, v_proj, short_weight, long_filter, long_bias, residual, norm_gain):
    tokens, channels = q_proj.shape
    pieces, groups = lax.axis_size("seq"), lax.axis_size("ch")
    own = channels // pieces
    block = (tokens, channels)
    operands = (
        q_proj, k_proj, v_proj, long_filter, residual, short_weight,
        long_bias.reshape(1, channels), norm_gain.reshape(1, channels),
    ) + constants
    scratch = [pltpu.VMEM(block, BF16) for _ in range(5)]
    scratch += [pltpu.VMEM(x.shape, x.dtype) for x in operands[5:]]
    scratch += [pltpu.VMEM((tokens + 8, channels), F32) for _ in range(3)]
    scratch += [pltpu.VMEM((8, channels), F32) for _ in range(2)]
    scratch += [pltpu.VMEM((channels, tokens), BF16) for _ in range(2)]
    scratch += [pltpu.VMEM((2, channels, tokens // 2), BF16) for _ in range(4)]
    scratch += [pltpu.VMEM(block, BF16)]
    scratch += [pltpu.VMEM((channels, tokens), F32) for _ in range(3)]
    scratch += [
        pltpu.VMEM((tokens // LANES, channels, LANES), F32),
        pltpu.VMEM((own * LANES, 2 * LANES), F32),
        pltpu.VMEM((tokens // LANES // 2, channels, LANES), F32),
        pltpu.VMEM((groups, 1, tokens), F32),
    ]
    scratch += [pltpu.SemaphoreType.DMA((count,)) for count in (14, 2, 5, 5, 2)]
    anywhere = pl.BlockSpec(memory_space=pl.ANY)
    operands = tuple(pltpu.with_memory_space_constraint(x, pltpu.HBM) for x in operands)
    both = pl.pallas_call(
        functools.partial(kernel, pieces, groups),
        out_shape=jax.ShapeDtypeStruct((2, *block), BF16),
        in_specs=[anywhere] * len(operands),
        out_specs=pl.BlockSpec(memory_space=pltpu.VMEM),
        scratch_shapes=scratch,
        compiler_params=pltpu.CompilerParams(
            collective_id=0, has_side_effects=True, vmem_limit_bytes=32 * 2**20
        ),
        cost_estimate=pl.CostEstimate(flops=1_300_000_000, bytes_accessed=4_000_000, transcendentals=0),
    )(*operands)
    return both[0], both[1]


def solution(mesh):
    pieces = mesh.shape["seq"]
    constants = tuple(jnp.asarray(x) for x in tables(pieces))
    placed = (
        P("seq", "ch"),
        P("seq", "ch"),
        P("seq", "ch"),
        P(None, None, "ch"),
        P("seq", "ch"),
        P("ch"),
        P("seq", "ch"),
        P("ch"),
    )
    return jax.shard_map(
        functools.partial(per_device, constants),
        mesh=mesh,
        in_specs=placed,
        out_specs=(P("seq", "ch"), P("seq", "ch")),
        check_vma=False,
    )
```

```python
import functools
import math

import jax
import jax.numpy as jnp
import ml_dtypes
import numpy as np
from jax import lax
from jax.experimental import pallas as pl
from jax.experimental.pallas import tpu as pltpu
from jax.sharding import PartitionSpec as P

D = 4096
MESH = pl.DeviceIdType.MESH
F32 = jnp.float32
BF16 = jnp.bfloat16
LANES = 128


def tables(pieces):
    n = LANES
    quarter = np.arange(n) + 0.25
    per = n // pieces
    rows = np.array([per * (r % pieces) + r // pieces for r in range(n)])
    angle = 2 * math.pi / n * (quarter[:, None] * rows[None, :] % n)
    first = np.concatenate([np.cos(angle), -np.sin(angle)], axis=0)
    last = np.concatenate([np.cos(angle.T), -np.sin(angle.T)], axis=1) / (n * n)
    points = np.arange(n)
    angle = 2 * math.pi / n * (points[:, None] * points[None, :] % n)
    cosine, sine = np.cos(angle), np.sin(angle)
    second = np.block([[cosine, -sine], [sine, cosine]])
    angle = 2 * math.pi / (n * n) * (quarter[:, None] * points[None, :])
    return (
        np.concatenate(halves(first), axis=1),
        np.stack(halves(second)),
        np.stack(halves(second.T.copy())),
        np.stack(halves(last)),
        np.cos(angle).astype(np.float32),
        np.sin(angle).astype(np.float32),
    )


def dot(left, right):
    return jnp.dot(left, right, preferred_element_type=F32)


def split(x):
    high = x.astype(BF16)
    return high, (x - high.astype(F32)).astype(BF16)


def halves(table):
    high = table.astype(ml_dtypes.bfloat16)
    return high, (table - high.astype(np.float64)).astype(ml_dtypes.bfloat16)


def order(step, count):
    half = (step + 1) // 2
    return lax.rem(count // 2 + jnp.where(lax.rem(step, 2) == 1, -half, half), count)


def kernel(
    pieces,
    groups,
    q_in, k_in, v_in, h_in, res_in, taps_in, bias_in, gain_in,
    first_in, second_in, third_in, last_in, cos_in, sin_in,
    both,
    q_b, k_b, v_b, h_b, res_b, taps, bias, gain,
    first, second, third, last, cos_t, sin_t,
    pad_q, pad_k, pad_v, halo_out, halo_in,
    h_send, h_recv, z_send, z_recv, y_send, y_recv, pregate_b,
    gate_t, skip_t, res_t, flat, spectrum_h, product, power_slots,
    load_sem, halo_sem, send_sem, recv_sem, power_sem,
):
    me, ch = lax.axis_index("seq"), lax.axis_index("ch")
    tokens, channels = h_b.shape
    own = channels // pieces
    blocks = tokens // LANES
    wide = channels // LANES
    line = 4
    rings = pieces // line

    def peer(step):
        z = lax.rem(me // line + order(step // line, rings), rings)
        y = lax.rem(lax.rem(me, line) + order(lax.rem(step, line), line), line)
        return z * line + y

    def early(step):
        z = lax.rem(step // line, 2) * (rings // 2) + step // (2 * line)
        y = lax.rem(step, line)
        return z * line + y

    pairs = [
        (h_in, h_b), (q_in, q_b), (k_in, k_b), (v_in, v_b), (taps_in, taps), (bias_in, bias), (first_in, first),
        (second_in, second), (third_in, third), (last_in, last), (cos_in, cos_t), (sin_in, sin_t),
        (res_in, res_b), (gain_in, gain),
    ]
    loads = [pltpu.make_async_copy(src, dst, load_sem.at[i]) for i, (src, dst) in enumerate(pairs)]
    for load in loads[:4]:
        load.start()

    barrier = pltpu.get_barrier_semaphore()

    def greet(step, _):
        pl.semaphore_signal(barrier, inc=1, device_id=(peer(step), ch), device_id_type=MESH)
        return 0

    lax.fori_loop(0, pieces - 1, greet, 0)

    def greet_row(d, _):
        pl.semaphore_signal(barrier, inc=1, device_id=(me, lax.rem(ch + d, groups)), device_id_type=MESH)
        return 0

    lax.fori_loop(1, groups, greet_row, 0)

    def tile(r, c):
        return slice(r * LANES, (r + 1) * LANES), slice(c * LANES, (c + 1) * LANES)

    for load in loads[4:]:
        load.start()

    loads[0].wait()
    for r in range(blocks):
        for c in range(wide):
            rows, cols = tile(r, c)
            h_send[cols, rows] = h_b[rows, cols].T

    for i in (1, 2, 3):
        loads[i].wait()
    tails = [x[tokens - 16 :, :].astype(F32)[14:, :] for x in (q_b, k_b, v_b)]
    halo_out[...] = jnp.concatenate(tails + [jnp.zeros((2, channels), F32)], axis=0)

    pl.semaphore_wait(barrier, pieces - 1 + groups - 1)

    halo_copy = pltpu.make_async_remote_copy(
        src_ref=halo_out, dst_ref=halo_in, send_sem=halo_sem.at[0], recv_sem=halo_sem.at[1],
        device_id=(lax.rem(me + 1, pieces), ch), device_id_type=MESH,
    )

    @pl.when(me < pieces - 1)
    def _():
        halo_copy.start()

    def send_all(source, target, slot, partner=peer):
        def send(step, _):
            other = partner(step)

            @pl.when(other != me)
            def _():
                pltpu.make_async_remote_copy(
                    src_ref=source.at[pl.ds(pl.multiple_of(other * own, own), own)],
                    dst_ref=target.at[pl.ds(pl.multiple_of(me * own, own), own)],
                    send_sem=send_sem.at[slot], recv_sem=recv_sem.at[slot],
                    device_id=(other, ch), device_id_type=MESH,
                ).start()

            return 0

        lax.fori_loop(0, pieces, send, 0)
        mine = pl.ds(pl.multiple_of(me * own, own), own)
        pltpu.make_async_copy(source.at[mine], target.at[mine], recv_sem.at[slot]).start()

    def wait_recv(target, slot):
        pltpu.make_async_copy(target, target, recv_sem.at[slot]).wait()

    def wait_send(source, slot):
        part = source.at[pl.ds(0, channels - own)]
        pltpu.make_async_copy(part, part, send_sem.at[slot]).wait()

    send_all(h_send, h_recv, 0)

    @pl.when(me == 0)
    def _():
        halo_in[...] = jnp.zeros_like(halo_in)

    for x, padded in ((k_b, pad_k), (v_b, pad_v), (q_b, pad_q)):
        padded[8:, :] = x[...].astype(F32)

    @pl.when(me > 0)
    def _():
        halo_copy.wait_recv()

    @pl.when(me < pieces - 1)
    def _():
        halo_copy.wait_send()

    for i, padded in enumerate((pad_q, pad_k, pad_v)):
        padded[6:8, :] = halo_in[2 * i : 2 * i + 2, :]

    for i in (4, 5):
        loads[i].wait()

    def short(s, padded, r, c):
        cols = tile(r, c)[1]
        total = taps[s, 0:1, cols] * padded[8 + r * LANES : 8 + (r + 1) * LANES, cols]
        total += taps[s, 1:2, cols] * padded[7 + r * LANES : 7 + (r + 1) * LANES, cols]
        return total + taps[s, 2:3, cols] * padded[6 + r * LANES : 6 + (r + 1) * LANES, cols]

    half = blocks // 2
    for r in range(half):
        for c in range(wide):
            parts = []
            for e in range(2):
                rows, cols = tile(r + e * half, c)
                pregate = (short(1, pad_k, r + e * half, c) * short(2, pad_v, r + e * half, c)).astype(BF16)
                pregate_b[rows, cols] = pregate
                parts.append(pregate.astype(F32).T.reshape(LANES // own, 2, own // 2, LANES))
            rows, cols = tile(r, c)
            for part in range(2):
                z_send[part, cols, rows] = (
                    jnp.stack([x[:, part] for x in parts], axis=1).reshape(LANES, LANES).astype(BF16)
                )

    send_all(z_send.at[0], z_recv.at[0], 1)

    loads[12].wait()
    for r in range(blocks):
        for c in range(wide):
            rows, cols = tile(r, c)
            gate_t[cols, rows] = short(0, pad_q, r, c).T
            skip_t[cols, rows] = (pregate_b[rows, cols].astype(F32) * bias[0:1, cols]).T
            res_t[cols, rows] = res_b[rows, cols].T.astype(F32)

    for i in (6, 7, 8, 9, 10, 11, 13):
        loads[i].wait()

    def product_of(x, table):
        high, low = split(x)
        return dot(high, table[0]) + (dot(low, table[0]) + dot(high, table[1]))

    def forward(signal):
        signal = jnp.concatenate(signal, axis=1).astype(BF16)
        partial = dot(first[...], jnp.concatenate([signal, signal], axis=0))
        turned = []
        for e in range(2):
            real = partial[:LANES, e * LANES : (e + 1) * LANES]
            imag = partial[LANES:, e * LANES : (e + 1) * LANES]
            cosine, sine = cos_t[...], sin_t[...]
            turned.append(
                jnp.concatenate([real * cosine + imag * sine, imag * cosine - real * sine], axis=1)
            )
        return product_of(jnp.concatenate(turned, axis=0), second)

    def widen(received, count):
        def step(r, _):
            rows = pl.ds(pl.multiple_of(r * 64, 64), 64)
            for i in range(count):
                flat[i, rows, :] = received[rows, i * LANES : (i + 1) * LANES].astype(F32)
            return 0

        lax.fori_loop(0, channels // 64, step, 0, unroll=4)

    wait_recv(h_recv, 0)
    widen(h_recv, blocks)

    def filter_step(p, _):
        signal = [
            jnp.concatenate([flat[i, pl.ds(2 * p + e, pieces, stride=own), :] for i in range(blocks)], axis=0)
            for e in range(2)
        ]
        spectrum_h[pl.ds(pl.multiple_of(p * 256, 256), 256), :] = forward(signal)
        return 0

    lax.fori_loop(0, own // 2, filter_step, 0, unroll=4)

    wait_send(z_send.at[0], 1)
    send_all(z_send.at[1], z_recv.at[1], 2)

    for part in range(2):
        wait_recv(z_recv.at[part], 1 + part)
        widen(z_recv.at[part], half)

        def signal_step(p, _):
            signal = [
                jnp.concatenate(
                    [
                        flat[i % half, pl.ds((i // half) * (own // 2) + 2 * p + e, pieces, stride=own), :]
                        for i in range(blocks)
                    ],
                    axis=0,
                )
                for e in range(2)
            ]
            x = forward(signal)
            w = spectrum_h[pl.ds(pl.multiple_of((part * own // 4 + p) * 256, 256), 256), :]
            xr, xi, wr, wi = x[:, :LANES], x[:, LANES:], w[:, :LANES], w[:, LANES:]
            both = jnp.concatenate([xr * wr - xi * wi, xr * wi + xi * wr], axis=1)
            back = product_of(both, third)
            turned = []
            for e in range(2):
                real = back[e * LANES : (e + 1) * LANES, :LANES]
                imag = back[e * LANES : (e + 1) * LANES, LANES:]
                cosine, sine = cos_t[...], sin_t[...]
                turned.append(
                    jnp.concatenate([real * cosine - imag * sine, real * sine + imag * cosine], axis=0)
                )
            high, low = split(jnp.concatenate(turned, axis=1))
            result = dot(last[0], high) + (dot(last[0], low) + dot(last[1], high))
            for e in range(2):
                for i in range(blocks):
                    product[i % half, pl.ds((i // half) * (own // 2) + 2 * p + e, pieces, stride=own), :] = result[
                        i * pieces : (i + 1) * pieces, e * LANES : (e + 1) * LANES
                    ]
            return 0

        lax.fori_loop(0, own // 4, signal_step, 0, unroll=4)

        def narrow(r, _):
            rows = pl.ds(pl.multiple_of(r * 64, 64), 64)
            for i in range(half):
                y_send[part, rows, i * LANES : (i + 1) * LANES] = product[i, rows, :].astype(BF16)
            return 0

        lax.fori_loop(0, channels // 64, narrow, 0, unroll=4)
        send_all(y_send.at[part], y_recv.at[part], 3 + part, early if part else peer)

    total = jnp.zeros((8, tokens), F32)
    for part in range(2):
        wait_recv(y_recv.at[part], 3 + part)

        def gate_step(j, total):
            conv = y_recv[part, pl.ds(pl.multiple_of(j * own, own), own), :].astype(F32)
            conv = jnp.concatenate([conv[: own // 2], conv[own // 2 :]], axis=1)
            rows = pl.ds(pl.multiple_of(j * own + part * (own // 2), 8), own // 2)
            mixed = (gate_t[rows, :] * (conv + skip_t[rows, :])).astype(BF16)
            stream = (res_t[rows, :] + mixed.astype(F32)).astype(BF16).astype(F32)
            res_t[rows, :] = stream
            return total + stream * stream

        total = lax.fori_loop(0, pieces, gate_step, total, unroll=8)
    power_slots[ch] = jnp.sum(total, axis=0, keepdims=True)

    def power_copy(d):
        other = lax.rem(ch + d, groups)
        return pltpu.make_async_remote_copy(
            src_ref=power_slots.at[ch], dst_ref=power_slots.at[ch],
            send_sem=power_sem.at[0], recv_sem=power_sem.at[1],
            device_id=(me, other), device_id_type=MESH,
        )

    for d in (4, 3, 5, 2, 6, 7, 1):
        power_copy(d).start()

    for r in range(blocks):
        for c in range(wide):
            rows, cols = tile(r, c)
            both[0, rows, cols] = res_t[cols, rows].T.astype(BF16)

    part = power_slots.at[pl.ds(0, groups - 1)]
    pltpu.make_async_copy(part, part, power_sem.at[1]).wait()
    power = jnp.sum(power_slots[...], axis=0) / D
    scale = lax.rsqrt(power + 1e-6)
    for r in range(blocks):
        rows = tile(r, 0)[0]
        column = jnp.broadcast_to(scale[:, rows], (LANES, LANES)).T
        for c in range(wide):
            cols = tile(r, c)[1]
            both[1, rows, cols] = (both[0, rows, cols].astype(F32) * column * gain[0:1, cols]).astype(BF16)

    pltpu.make_async_copy(part, part, power_sem.at[0]).wait()
    wait_send(h_send, 0)
    wait_send(z_send.at[1], 2)
    for part in range(2):
        wait_send(y_send.at[part], 3 + part)


def per_device(constants, q_proj, k_proj, v_proj, short_weight, long_filter, long_bias, residual, norm_gain):
    tokens, channels = q_proj.shape
    pieces, groups = lax.axis_size("seq"), lax.axis_size("ch")
    own = channels // pieces
    block = (tokens, channels)
    operands = (
        q_proj, k_proj, v_proj, long_filter, residual, short_weight,
        long_bias.reshape(1, channels), norm_gain.reshape(1, channels),
    ) + constants
    scratch = [pltpu.VMEM(block, BF16) for _ in range(5)]
    scratch += [pltpu.VMEM(x.shape, x.dtype) for x in operands[5:]]
    scratch += [pltpu.VMEM((tokens + 8, channels), F32) for _ in range(3)]
    scratch += [pltpu.VMEM((8, channels), F32) for _ in range(2)]
    scratch += [pltpu.VMEM((channels, tokens), BF16) for _ in range(2)]
    scratch += [pltpu.VMEM((2, channels, tokens // 2), BF16) for _ in range(4)]
    scratch += [pltpu.VMEM(block, BF16)]
    scratch += [pltpu.VMEM((channels, tokens), F32) for _ in range(3)]
    scratch += [
        pltpu.VMEM((tokens // LANES, channels, LANES), F32),
        pltpu.VMEM((own * LANES, 2 * LANES), F32),
        pltpu.VMEM((tokens // LANES // 2, channels, LANES), F32),
        pltpu.VMEM((groups, 1, tokens), F32),
    ]
    scratch += [pltpu.SemaphoreType.DMA((count,)) for count in (14, 2, 5, 5, 2)]
    anywhere = pl.BlockSpec(memory_space=pl.ANY)
    operands = tuple(pltpu.with_memory_space_constraint(x, pltpu.HBM) for x in operands)
    both = pl.pallas_call(
        functools.partial(kernel, pieces, groups),
        out_shape=jax.ShapeDtypeStruct((2, *block), BF16),
        in_specs=[anywhere] * len(operands),
        out_specs=pl.BlockSpec(memory_space=pltpu.VMEM),
        scratch_shapes=scratch,
        compiler_params=pltpu.CompilerParams(
            collective_id=0, has_side_effects=True, vmem_limit_bytes=32 * 2**20
        ),
        cost_estimate=pl.CostEstimate(flops=1_300_000_000, bytes_accessed=4_000_000, transcendentals=0),
    )(*operands)
    return both[0], both[1]


def solution(mesh):
    pieces = mesh.shape["seq"]
    constants = tuple(jnp.asarray(x) for x in tables(pieces))
    placed = (
        P("seq", "ch"),
        P("seq", "ch"),
        P("seq", "ch"),
        P(None, None, "ch"),
        P("seq", "ch"),
        P("ch"),
        P("seq", "ch"),
        P("ch"),
    )
    return jax.shard_map(
        functools.partial(per_device, constants),
        mesh=mesh,
        in_specs=placed,
        out_specs=(P("seq", "ch"), P("seq", "ch")),
        check_vma=False,
    )
```

```python
import functools
import math

import jax
import jax.numpy as jnp
import ml_dtypes
import numpy as np
from jax import lax
from jax.experimental import pallas as pl
from jax.experimental.pallas import tpu as pltpu
from jax.sharding import PartitionSpec as P

D = 4096
MESH = pl.DeviceIdType.MESH
F32 = jnp.float32
BF16 = jnp.bfloat16
LANES = 128


def tables(pieces):
    n = LANES
    quarter = np.arange(n) + 0.25
    per = n // pieces
    rows = np.array([per * (r % pieces) + r // pieces for r in range(n)])
    angle = 2 * math.pi / n * (quarter[:, None] * rows[None, :] % n)
    first = np.concatenate([np.cos(angle), -np.sin(angle)], axis=0)
    last = np.concatenate([np.cos(angle.T), -np.sin(angle.T)], axis=1) / (n * n)
    points = np.arange(n)
    angle = 2 * math.pi / n * (points[:, None] * points[None, :] % n)
    cosine, sine = np.cos(angle), np.sin(angle)
    second = np.block([[cosine, -sine], [sine, cosine]])
    angle = 2 * math.pi / (n * n) * (quarter[:, None] * points[None, :])
    return (
        np.concatenate(halves(first), axis=1),
        np.stack(halves(second)),
        np.stack(halves(second.T.copy())),
        np.stack(halves(last)),
        np.cos(angle).astype(np.float32),
        np.sin(angle).astype(np.float32),
    )


def dot(left, right):
    return jnp.dot(left, right, preferred_element_type=F32)


def split(x):
    high = x.astype(BF16)
    return high, (x - high.astype(F32)).astype(BF16)


def halves(table):
    high = table.astype(ml_dtypes.bfloat16)
    return high, (table - high.astype(np.float64)).astype(ml_dtypes.bfloat16)


def order(step, count):
    half = (step + 1) // 2
    return lax.rem(count // 2 + jnp.where(lax.rem(step, 2) == 1, -half, half), count)


def kernel(
    pieces,
    groups,
    q_in, k_in, v_in, h_in, res_in, taps_in, bias_in, gain_in,
    first_in, second_in, third_in, last_in, cos_in, sin_in,
    both,
    q_b, k_b, v_b, h_b, res_b, taps, bias, gain,
    first, second, third, last, cos_t, sin_t,
    pad_q, pad_k, pad_v, halo_out, halo_in,
    h_send, h_recv, z_send, z_recv, y_send, y_recv, pregate_b,
    gate_t, skip_t, res_t, flat, spectrum_h, product, power_slots,
    load_sem, halo_sem, send_sem, recv_sem, power_sem,
):
    me, ch = lax.axis_index("seq"), lax.axis_index("ch")
    tokens, channels = h_b.shape
    own = channels // pieces
    blocks = tokens // LANES
    wide = channels // LANES
    line = 4
    rings = pieces // line

    def peer(step):
        z = lax.rem(me // line + order(step // line, rings), rings)
        y = lax.rem(lax.rem(me, line) + order(lax.rem(step, line), line), line)
        return z * line + y

    def early(step):
        z = lax.rem(step // line, 2) * (rings // 2) + step // (2 * line)
        y = lax.rem(step, line)
        return z * line + y

    pairs = [
        (h_in, h_b), (q_in, q_b), (k_in, k_b), (v_in, v_b), (taps_in, taps), (bias_in, bias), (first_in, first),
        (second_in, second), (third_in, third), (last_in, last), (cos_in, cos_t), (sin_in, sin_t),
        (res_in, res_b), (gain_in, gain),
    ]
    loads = [pltpu.make_async_copy(src, dst, load_sem.at[i]) for i, (src, dst) in enumerate(pairs)]

    barrier = pltpu.get_barrier_semaphore()

    def greet(step, _):
        pl.semaphore_signal(
            barrier, inc=1, device_id=(step + jnp.where(step >= me, 1, 0), ch), device_id_type=MESH
        )
        return 0

    lax.fori_loop(0, pieces - 1, greet, 0)

    def greet_row(d, _):
        pl.semaphore_signal(barrier, inc=1, device_id=(me, lax.rem(ch + d, groups)), device_id_type=MESH)
        return 0

    lax.fori_loop(1, groups, greet_row, 0)

    def tile(r, c):
        return slice(r * LANES, (r + 1) * LANES), slice(c * LANES, (c + 1) * LANES)

    for load in loads:
        load.start()

    loads[0].wait()
    for r in range(blocks):
        for c in range(wide):
            rows, cols = tile(r, c)
            h_send[cols, rows] = h_b[rows, cols].T

    for i in (1, 2, 3):
        loads[i].wait()
    tails = [x[tokens - 16 :, :].astype(F32)[14:, :] for x in (q_b, k_b, v_b)]
    halo_out[...] = jnp.concatenate(tails + [jnp.zeros((2, channels), F32)], axis=0)

    pl.semaphore_wait(barrier, pieces - 1 + groups - 1)

    halo_copy = pltpu.make_async_remote_copy(
        src_ref=halo_out, dst_ref=halo_in, send_sem=halo_sem.at[0], recv_sem=halo_sem.at[1],
        device_id=(lax.rem(me + 1, pieces), ch), device_id_type=MESH,
    )

    @pl.when(me < pieces - 1)
    def _():
        halo_copy.start()

    def send_all(source, target, slot, partner=peer):
        def send(step, _):
            other = partner(step)

            @pl.when(other != me)
            def _():
                pltpu.make_async_remote_copy(
                    src_ref=source.at[pl.ds(pl.multiple_of(other * own, own), own)],
                    dst_ref=target.at[pl.ds(pl.multiple_of(me * own, own), own)],
                    send_sem=send_sem.at[slot], recv_sem=recv_sem.at[slot],
                    device_id=(other, ch), device_id_type=MESH,
                ).start()

            return 0

        lax.fori_loop(0, pieces, send, 0)
        mine = pl.ds(pl.multiple_of(me * own, own), own)
        pltpu.make_async_copy(source.at[mine], target.at[mine], recv_sem.at[slot]).start()

    def wait_recv(target, slot):
        pltpu.make_async_copy(target, target, recv_sem.at[slot]).wait()

    def wait_send(source, slot):
        part = source.at[pl.ds(0, channels - own)]
        pltpu.make_async_copy(part, part, send_sem.at[slot]).wait()

    send_all(h_send, h_recv, 0)

    @pl.when(me == 0)
    def _():
        halo_in[...] = jnp.zeros_like(halo_in)

    for x, padded in ((k_b, pad_k), (v_b, pad_v), (q_b, pad_q)):
        padded[8:, :] = x[...].astype(F32)

    @pl.when(me > 0)
    def _():
        halo_copy.wait_recv()

    @pl.when(me < pieces - 1)
    def _():
        halo_copy.wait_send()

    for i, padded in enumerate((pad_q, pad_k, pad_v)):
        padded[6:8, :] = halo_in[2 * i : 2 * i + 2, :]

    for i in (4, 5):
        loads[i].wait()

    def short(s, padded, r, c):
        cols = tile(r, c)[1]
        total = taps[s, 0:1, cols] * padded[8 + r * LANES : 8 + (r + 1) * LANES, cols]
        total += taps[s, 1:2, cols] * padded[7 + r * LANES : 7 + (r + 1) * LANES, cols]
        return total + taps[s, 2:3, cols] * padded[6 + r * LANES : 6 + (r + 1) * LANES, cols]

    half = blocks // 2
    for r in range(half):
        for c in range(wide):
            parts = []
            for e in range(2):
                rows, cols = tile(r + e * half, c)
                pregate = (short(1, pad_k, r + e * half, c) * short(2, pad_v, r + e * half, c)).astype(BF16)
                pregate_b[rows, cols] = pregate
                parts.append(pregate.astype(F32).T.reshape(LANES // own, 2, own // 2, LANES))
            rows, cols = tile(r, c)
            for part in range(2):
                z_send[part, cols, rows] = (
                    jnp.stack([x[:, part] for x in parts], axis=1).reshape(LANES, LANES).astype(BF16)
                )

    send_all(z_send.at[0], z_recv.at[0], 1)

    loads[12].wait()
    for r in range(blocks):
        for c in range(wide):
            rows, cols = tile(r, c)
            gate_t[cols, rows] = short(0, pad_q, r, c).T
            skip_t[cols, rows] = (pregate_b[rows, cols].astype(F32) * bias[0:1, cols]).T
            res_t[cols, rows] = res_b[rows, cols].T.astype(F32)

    for i in (6, 7, 8, 9, 10, 11, 13):
        loads[i].wait()

    def product_of(x, table):
        high, low = split(x)
        return dot(high, table[0]) + (dot(low, table[0]) + dot(high, table[1]))

    def forward(signal):
        signal = jnp.concatenate(signal, axis=1).astype(BF16)
        partial = dot(first[...], jnp.concatenate([signal, signal], axis=0))
        turned = []
        for e in range(2):
            real = partial[:LANES, e * LANES : (e + 1) * LANES]
            imag = partial[LANES:, e * LANES : (e + 1) * LANES]
            cosine, sine = cos_t[...], sin_t[...]
            turned.append(
                jnp.concatenate([real * cosine + imag * sine, imag * cosine - real * sine], axis=1)
            )
        return product_of(jnp.concatenate(turned, axis=0), second)

    def widen(received, count):
        def step(r, _):
            rows = pl.ds(pl.multiple_of(r * 64, 64), 64)
            for i in range(count):
                flat[i, rows, :] = received[rows, i * LANES : (i + 1) * LANES].astype(F32)
            return 0

        lax.fori_loop(0, channels // 64, step, 0, unroll=4)

    wait_recv(h_recv, 0)
    widen(h_recv, blocks)

    def filter_step(p, _):
        signal = [
            jnp.concatenate([flat[i, pl.ds(2 * p + e, pieces, stride=own), :] for i in range(blocks)], axis=0)
            for e in range(2)
        ]
        spectrum_h[pl.ds(pl.multiple_of(p * 256, 256), 256), :] = forward(signal)
        return 0

    lax.fori_loop(0, own // 2, filter_step, 0, unroll=4)

    wait_send(z_send.at[0], 1)
    send_all(z_send.at[1], z_recv.at[1], 2)

    for part in range(2):
        wait_recv(z_recv.at[part], 1 + part)
        widen(z_recv.at[part], half)

        def signal_step(p, _):
            signal = [
                jnp.concatenate(
                    [
                        flat[i % half, pl.ds((i // half) * (own // 2) + 2 * p + e, pieces, stride=own), :]
                        for i in range(blocks)
                    ],
                    axis=0,
                )
                for e in range(2)
            ]
            x = forward(signal)
            w = spectrum_h[pl.ds(pl.multiple_of((part * own // 4 + p) * 256, 256), 256), :]
            xr, xi, wr, wi = x[:, :LANES], x[:, LANES:], w[:, :LANES], w[:, LANES:]
            both = jnp.concatenate([xr * wr - xi * wi, xr * wi + xi * wr], axis=1)
            back = product_of(both, third)
            turned = []
            for e in range(2):
                real = back[e * LANES : (e + 1) * LANES, :LANES]
                imag = back[e * LANES : (e + 1) * LANES, LANES:]
                cosine, sine = cos_t[...], sin_t[...]
                turned.append(
                    jnp.concatenate([real * cosine - imag * sine, real * sine + imag * cosine], axis=0)
                )
            high, low = split(jnp.concatenate(turned, axis=1))
            result = dot(last[0], high) + (dot(last[0], low) + dot(last[1], high))
            for e in range(2):
                for i in range(blocks):
                    product[i % half, pl.ds((i // half) * (own // 2) + 2 * p + e, pieces, stride=own), :] = result[
                        i * pieces : (i + 1) * pieces, e * LANES : (e + 1) * LANES
                    ]
            return 0

        lax.fori_loop(0, own // 4, signal_step, 0, unroll=4)

        def narrow(r, _):
            rows = pl.ds(pl.multiple_of(r * 64, 64), 64)
            for i in range(half):
                y_send[part, rows, i * LANES : (i + 1) * LANES] = product[i, rows, :].astype(BF16)
            return 0

        lax.fori_loop(0, channels // 64, narrow, 0, unroll=4)
        send_all(y_send.at[part], y_recv.at[part], 3 + part, early if part else peer)

    total = jnp.zeros((8, tokens), F32)
    for part in range(2):
        wait_recv(y_recv.at[part], 3 + part)

        def gate_step(j, total):
            conv = y_recv[part, pl.ds(pl.multiple_of(j * own, own), own), :].astype(F32)
            conv = jnp.concatenate([conv[: own // 2], conv[own // 2 :]], axis=1)
            rows = pl.ds(pl.multiple_of(j * own + part * (own // 2), 8), own // 2)
            mixed = (gate_t[rows, :] * (conv + skip_t[rows, :])).astype(BF16)
            stream = (res_t[rows, :] + mixed.astype(F32)).astype(BF16).astype(F32)
            res_t[rows, :] = stream
            return total + stream * stream

        total = lax.fori_loop(0, pieces, gate_step, total, unroll=8)
    power_slots[ch] = jnp.sum(total, axis=0, keepdims=True)

    def power_copy(d):
        other = lax.rem(ch + d, groups)
        return pltpu.make_async_remote_copy(
            src_ref=power_slots.at[ch], dst_ref=power_slots.at[ch],
            send_sem=power_sem.at[0], recv_sem=power_sem.at[1],
            device_id=(me, other), device_id_type=MESH,
        )

    for d in (4, 3, 5, 2, 6, 7, 1):
        power_copy(d).start()

    for r in range(blocks):
        for c in range(wide):
            rows, cols = tile(r, c)
            both[0, rows, cols] = res_t[cols, rows].T.astype(BF16)

    part = power_slots.at[pl.ds(0, groups - 1)]
    pltpu.make_async_copy(part, part, power_sem.at[1]).wait()
    power = jnp.sum(power_slots[...], axis=0) / D
    scale = lax.rsqrt(power + 1e-6)
    for r in range(blocks):
        rows = tile(r, 0)[0]
        column = jnp.broadcast_to(scale[:, rows], (LANES, LANES)).T
        for c in range(wide):
            cols = tile(r, c)[1]
            both[1, rows, cols] = (both[0, rows, cols].astype(F32) * column * gain[0:1, cols]).astype(BF16)

    pltpu.make_async_copy(part, part, power_sem.at[0]).wait()
    wait_send(h_send, 0)
    wait_send(z_send.at[1], 2)
    for part in range(2):
        wait_send(y_send.at[part], 3 + part)


def per_device(constants, q_proj, k_proj, v_proj, short_weight, long_filter, long_bias, residual, norm_gain):
    tokens, channels = q_proj.shape
    pieces, groups = lax.axis_size("seq"), lax.axis_size("ch")
    own = channels // pieces
    block = (tokens, channels)
    operands = (
        q_proj, k_proj, v_proj, long_filter, residual, short_weight,
        long_bias.reshape(1, channels), norm_gain.reshape(1, channels),
    ) + constants
    scratch = [pltpu.VMEM(block, BF16) for _ in range(5)]
    scratch += [pltpu.VMEM(x.shape, x.dtype) for x in operands[5:]]
    scratch += [pltpu.VMEM((tokens + 8, channels), F32) for _ in range(3)]
    scratch += [pltpu.VMEM((8, channels), F32) for _ in range(2)]
    scratch += [pltpu.VMEM((channels, tokens), BF16) for _ in range(2)]
    scratch += [pltpu.VMEM((2, channels, tokens // 2), BF16) for _ in range(4)]
    scratch += [pltpu.VMEM(block, BF16)]
    scratch += [pltpu.VMEM((channels, tokens), F32) for _ in range(3)]
    scratch += [
        pltpu.VMEM((tokens // LANES, channels, LANES), F32),
        pltpu.VMEM((own * LANES, 2 * LANES), F32),
        pltpu.VMEM((tokens // LANES // 2, channels, LANES), F32),
        pltpu.VMEM((groups, 1, tokens), F32),
    ]
    scratch += [pltpu.SemaphoreType.DMA((count,)) for count in (14, 2, 5, 5, 2)]
    anywhere = pl.BlockSpec(memory_space=pl.ANY)
    operands = tuple(pltpu.with_memory_space_constraint(x, pltpu.HBM) for x in operands)
    both = pl.pallas_call(
        functools.partial(kernel, pieces, groups),
        out_shape=jax.ShapeDtypeStruct((2, *block), BF16),
        in_specs=[anywhere] * len(operands),
        out_specs=pl.BlockSpec(memory_space=pltpu.VMEM),
        scratch_shapes=scratch,
        compiler_params=pltpu.CompilerParams(
            collective_id=0, has_side_effects=True, vmem_limit_bytes=32 * 2**20
        ),
        cost_estimate=pl.CostEstimate(flops=1_300_000_000, bytes_accessed=4_000_000, transcendentals=0),
    )(*operands)
    return both[0], both[1]


def solution(mesh):
    pieces = mesh.shape["seq"]
    constants = tuple(jnp.asarray(x) for x in tables(pieces))
    placed = (
        P("seq", "ch"),
        P("seq", "ch"),
        P("seq", "ch"),
        P(None, None, "ch"),
        P("seq", "ch"),
        P("ch"),
        P("seq", "ch"),
        P("ch"),
    )
    return jax.shard_map(
        functools.partial(per_device, constants),
        mesh=mesh,
        in_specs=placed,
        out_specs=(P("seq", "ch"), P("seq", "ch")),
        check_vma=False,
    )
```

```python
import functools
import math

import jax
import jax.numpy as jnp
import ml_dtypes
import numpy as np
from jax import lax
from jax.experimental import pallas as pl
from jax.experimental.pallas import tpu as pltpu
from jax.sharding import PartitionSpec as P

D = 4096
MESH = pl.DeviceIdType.MESH
F32 = jnp.float32
BF16 = jnp.bfloat16
LANES = 128


def tables(pieces):
    n = LANES
    quarter = np.arange(n) + 0.25
    per = n // pieces
    rows = np.array([per * (r % pieces) + r // pieces for r in range(n)])
    angle = 2 * math.pi / n * (quarter[:, None] * rows[None, :] % n)
    first = np.concatenate([np.cos(angle), -np.sin(angle)], axis=0)
    last = np.concatenate([np.cos(angle.T), -np.sin(angle.T)], axis=1) / (n * n)
    points = np.arange(n)
    angle = 2 * math.pi / n * (points[:, None] * points[None, :] % n)
    cosine, sine = np.cos(angle), np.sin(angle)
    second = np.block([[cosine, -sine], [sine, cosine]])
    angle = 2 * math.pi / (n * n) * (quarter[:, None] * points[None, :])
    return (
        np.concatenate(halves(first), axis=1),
        np.stack(halves(second)),
        np.stack(halves(second.T.copy())),
        np.stack(halves(last)),
        np.cos(angle).astype(np.float32),
        np.sin(angle).astype(np.float32),
    )


def dot(left, right):
    return jnp.dot(left, right, preferred_element_type=F32)


def split(x):
    high = x.astype(BF16)
    return high, (x - high.astype(F32)).astype(BF16)


def halves(table):
    high = table.astype(ml_dtypes.bfloat16)
    return high, (table - high.astype(np.float64)).astype(ml_dtypes.bfloat16)


def order(step, count):
    half = (step + 1) // 2
    return lax.rem(count // 2 + jnp.where(lax.rem(step, 2) == 1, -half, half), count)


def kernel(
    pieces,
    groups,
    q_in, k_in, v_in, h_in, res_in, taps_in, bias_in, gain_in,
    first_in, second_in, third_in, last_in, cos_in, sin_in,
    both,
    q_b, k_b, v_b, h_b, res_b, taps, bias, gain,
    first, second, third, last, cos_t, sin_t,
    pad_q, pad_k, pad_v, halo_out, halo_in,
    h_send, h_recv, z_send, z_recv, y_send, y_recv, pregate_b,
    gate_t, skip_t, res_t, flat, spectrum_h, product, power_slots,
    load_sem, halo_sem, send_sem, recv_sem, power_sem,
):
    me, ch = lax.axis_index("seq"), lax.axis_index("ch")
    tokens, channels = h_b.shape
    own = channels // pieces
    blocks = tokens // LANES
    wide = channels // LANES
    line = 4
    rings = pieces // line

    def peer(step):
        z = lax.rem(me // line + order(step // line, rings), rings)
        y = lax.rem(lax.rem(me, line) + order(lax.rem(step, line), line), line)
        return z * line + y

    def early(step):
        z = lax.rem(step // line, 2) * (rings // 2) + step // (2 * line)
        y = lax.rem(step, line)
        return z * line + y

    pairs = [
        (h_in, h_b), (q_in, q_b), (k_in, k_b), (v_in, v_b), (taps_in, taps), (bias_in, bias), (first_in, first),
        (second_in, second), (third_in, third), (last_in, last), (cos_in, cos_t), (sin_in, sin_t),
        (res_in, res_b), (gain_in, gain),
    ]
    loads = [pltpu.make_async_copy(src, dst, load_sem.at[i]) for i, (src, dst) in enumerate(pairs)]

    barrier = pltpu.get_barrier_semaphore()

    def greet(step, _):
        pl.semaphore_signal(
            barrier, inc=1, device_id=(step + jnp.where(step >= me, 1, 0), ch), device_id_type=MESH
        )
        return 0

    lax.fori_loop(0, pieces - 1, greet, 0)

    def greet_row(d, _):
        pl.semaphore_signal(barrier, inc=1, device_id=(me, lax.rem(ch + d, groups)), device_id_type=MESH)
        return 0

    lax.fori_loop(1, groups, greet_row, 0)

    def tile(r, c):
        return slice(r * LANES, (r + 1) * LANES), slice(c * LANES, (c + 1) * LANES)

    for load in loads:
        load.start()

    loads[0].wait()
    for r in range(blocks):
        for c in range(wide):
            rows, cols = tile(r, c)
            h_send[cols, rows] = h_b[rows, cols].T

    for i in (1, 2, 3):
        loads[i].wait()
    tails = [x[tokens - 16 :, :].astype(F32)[14:, :] for x in (q_b, k_b, v_b)]
    halo_out[...] = jnp.concatenate(tails + [jnp.zeros((2, channels), F32)], axis=0)

    pl.semaphore_wait(barrier, pieces - 1 + groups - 1)

    halo_copy = pltpu.make_async_remote_copy(
        src_ref=halo_out, dst_ref=halo_in, send_sem=halo_sem.at[0], recv_sem=halo_sem.at[1],
        device_id=(lax.rem(me + 1, pieces), ch), device_id_type=MESH,
    )

    @pl.when(me < pieces - 1)
    def _():
        halo_copy.start()

    def send_all(source, target, slot, partner=peer):
        def send(step, _):
            other = partner(step)

            @pl.when(other != me)
            def _():
                pltpu.make_async_remote_copy(
                    src_ref=source.at[pl.ds(pl.multiple_of(other * own, own), own)],
                    dst_ref=target.at[pl.ds(pl.multiple_of(me * own, own), own)],
                    send_sem=send_sem.at[slot], recv_sem=recv_sem.at[slot],
                    device_id=(other, ch), device_id_type=MESH,
                ).start()

            return 0

        lax.fori_loop(0, pieces, send, 0)
        mine = pl.ds(pl.multiple_of(me * own, own), own)
        pltpu.make_async_copy(source.at[mine], target.at[mine], recv_sem.at[slot]).start()

    def wait_recv(target, slot):
        pltpu.make_async_copy(target, target, recv_sem.at[slot]).wait()

    def wait_send(source, slot):
        part = source.at[pl.ds(0, channels - own)]
        pltpu.make_async_copy(part, part, send_sem.at[slot]).wait()

    send_all(h_send, h_recv, 0)

    @pl.when(me == 0)
    def _():
        halo_in[...] = jnp.zeros_like(halo_in)

    for x, padded in ((k_b, pad_k), (v_b, pad_v), (q_b, pad_q)):
        padded[8:, :] = x[...].astype(F32)

    @pl.when(me > 0)
    def _():
        halo_copy.wait_recv()

    @pl.when(me < pieces - 1)
    def _():
        halo_copy.wait_send()

    for i, padded in enumerate((pad_q, pad_k, pad_v)):
        padded[6:8, :] = halo_in[2 * i : 2 * i + 2, :]

    for i in (4, 5):
        loads[i].wait()

    def short(s, padded, r, c):
        cols = tile(r, c)[1]
        total = taps[s, 0:1, cols] * padded[8 + r * LANES : 8 + (r + 1) * LANES, cols]
        total += taps[s, 1:2, cols] * padded[7 + r * LANES : 7 + (r + 1) * LANES, cols]
        return total + taps[s, 2:3, cols] * padded[6 + r * LANES : 6 + (r + 1) * LANES, cols]

    half = blocks // 2
    for r in range(half):
        for c in range(wide):
            parts = []
            for e in range(2):
                rows, cols = tile(r + e * half, c)
                pregate = (short(1, pad_k, r + e * half, c) * short(2, pad_v, r + e * half, c)).astype(BF16)
                pregate_b[rows, cols] = pregate
                parts.append(pregate.astype(F32).T.reshape(LANES // own, 2, own // 2, LANES))
            rows, cols = tile(r, c)
            for part in range(2):
                z_send[part, cols, rows] = (
                    jnp.stack([x[:, part] for x in parts], axis=1).reshape(LANES, LANES).astype(BF16)
                )

    send_all(z_send.at[0], z_recv.at[0], 1)

    loads[12].wait()
    for r in range(blocks):
        for c in range(wide):
            rows, cols = tile(r, c)
            gate_t[cols, rows] = short(0, pad_q, r, c).T
            skip_t[cols, rows] = (pregate_b[rows, cols].astype(F32) * bias[0:1, cols]).T
            res_t[cols, rows] = res_b[rows, cols].T.astype(F32)

    for i in (6, 7, 8, 9, 10, 11, 13):
        loads[i].wait()

    def product_of(x, table):
        high, low = split(x)
        return dot(high, table[0]) + (dot(low, table[0]) + dot(high, table[1]))

    def forward(signal):
        signal = jnp.concatenate(signal, axis=1).astype(BF16)
        partial = dot(first[...], jnp.concatenate([signal, signal], axis=0))
        turned = []
        for e in range(2):
            real = partial[:LANES, e * LANES : (e + 1) * LANES]
            imag = partial[LANES:, e * LANES : (e + 1) * LANES]
            cosine, sine = cos_t[...], sin_t[...]
            turned.append(
                jnp.concatenate([real * cosine + imag * sine, imag * cosine - real * sine], axis=1)
            )
        return product_of(jnp.concatenate(turned, axis=0), second)

    def widen(received, count):
        def step(r, _):
            rows = pl.ds(pl.multiple_of(r * 64, 64), 64)
            for i in range(count):
                flat[i, rows, :] = received[rows, i * LANES : (i + 1) * LANES].astype(F32)
            return 0

        lax.fori_loop(0, channels // 64, step, 0, unroll=4)

    wait_recv(h_recv, 0)
    widen(h_recv, blocks)

    def filter_step(p, _):
        signal = [
            jnp.concatenate([flat[i, pl.ds(2 * p + e, pieces, stride=own), :] for i in range(blocks)], axis=0)
            for e in range(2)
        ]
        spectrum_h[pl.ds(pl.multiple_of(p * 256, 256), 256), :] = forward(signal)
        return 0

    lax.fori_loop(0, own // 2, filter_step, 0, unroll=4)

    wait_send(z_send.at[0], 1)
    send_all(z_send.at[1], z_recv.at[1], 2)

    for part in range(2):
        wait_recv(z_recv.at[part], 1 + part)
        widen(z_recv.at[part], half)

        def signal_step(p, _):
            signal = [
                jnp.concatenate(
                    [
                        flat[i % half, pl.ds((i // half) * (own // 2) + 2 * p + e, pieces, stride=own), :]
                        for i in range(blocks)
                    ],
                    axis=0,
                )
                for e in range(2)
            ]
            x = forward(signal)
            w = spectrum_h[pl.ds(pl.multiple_of((part * own // 4 + p) * 256, 256), 256), :]
            xr, xi, wr, wi = x[:, :LANES], x[:, LANES:], w[:, :LANES], w[:, LANES:]
            both = jnp.concatenate([xr * wr - xi * wi, xr * wi + xi * wr], axis=1)
            back = product_of(both, third)
            turned = []
            for e in range(2):
                real = back[e * LANES : (e + 1) * LANES, :LANES]
                imag = back[e * LANES : (e + 1) * LANES, LANES:]
                cosine, sine = cos_t[...], sin_t[...]
                turned.append(
                    jnp.concatenate([real * cosine - imag * sine, real * sine + imag * cosine], axis=0)
                )
            high, low = split(jnp.concatenate(turned, axis=1))
            result = dot(last[0], high) + (dot(last[0], low) + dot(last[1], high))
            for e in range(2):
                for i in range(blocks):
                    product[i % half, pl.ds((i // half) * (own // 2) + 2 * p + e, pieces, stride=own), :] = result[
                        i * pieces : (i + 1) * pieces, e * LANES : (e + 1) * LANES
                    ]
            return 0

        lax.fori_loop(0, own // 4, signal_step, 0, unroll=4)

        def narrow(r, _):
            rows = pl.ds(pl.multiple_of(r * 64, 64), 64)
            for i in range(half):
                y_send[part, rows, i * LANES : (i + 1) * LANES] = product[i, rows, :].astype(BF16)
            return 0

        lax.fori_loop(0, channels // 64, narrow, 0, unroll=4)
        send_all(y_send.at[part], y_recv.at[part], 3 + part, early if part else peer)

    total = jnp.zeros((8, tokens), F32)
    for part in range(2):
        wait_recv(y_recv.at[part], 3 + part)

        def gate_step(j, total):
            conv = y_recv[part, pl.ds(pl.multiple_of(j * own, own), own), :].astype(F32)
            conv = jnp.concatenate([conv[: own // 2], conv[own // 2 :]], axis=1)
            rows = pl.ds(pl.multiple_of(j * own + part * (own // 2), 8), own // 2)
            mixed = (gate_t[rows, :] * (conv + skip_t[rows, :])).astype(BF16)
            stream = (res_t[rows, :] + mixed.astype(F32)).astype(BF16).astype(F32)
            res_t[rows, :] = stream
            return total + stream * stream

        total = lax.fori_loop(0, pieces, gate_step, total, unroll=8)
    power_slots[ch] = jnp.sum(total, axis=0, keepdims=True)

    def power_copy(d):
        other = lax.rem(ch + d, groups)
        return pltpu.make_async_remote_copy(
            src_ref=power_slots.at[ch], dst_ref=power_slots.at[ch],
            send_sem=power_sem.at[0], recv_sem=power_sem.at[1],
            device_id=(me, other), device_id_type=MESH,
        )

    for d in (4, 3, 5, 2, 6, 7, 1):
        power_copy(d).start()

    for r in range(blocks):
        for c in range(wide):
            rows, cols = tile(r, c)
            both[0, rows, cols] = res_t[cols, rows].T.astype(BF16)

    part = power_slots.at[pl.ds(0, groups - 1)]
    pltpu.make_async_copy(part, part, power_sem.at[1]).wait()
    power = jnp.sum(power_slots[...], axis=0) / D
    scale = lax.rsqrt(power + 1e-6)
    for r in range(blocks):
        rows = tile(r, 0)[0]
        column = jnp.broadcast_to(scale[:, rows], (LANES, LANES)).T
        for c in range(wide):
            cols = tile(r, c)[1]
            both[1, rows, cols] = (both[0, rows, cols].astype(F32) * column * gain[0:1, cols]).astype(BF16)

    pltpu.make_async_copy(part, part, power_sem.at[0]).wait()
    wait_send(h_send, 0)
    wait_send(z_send.at[1], 2)
    for part in range(2):
        wait_send(y_send.at[part], 3 + part)


def per_device(constants, q_proj, k_proj, v_proj, short_weight, long_filter, long_bias, residual, norm_gain):
    tokens, channels = q_proj.shape
    pieces, groups = lax.axis_size("seq"), lax.axis_size("ch")
    own = channels // pieces
    block = (tokens, channels)
    operands = (
        q_proj, k_proj, v_proj, long_filter, residual, short_weight,
        long_bias.reshape(1, channels), norm_gain.reshape(1, channels),
    ) + constants
    scratch = [pltpu.VMEM(block, BF16) for _ in range(5)]
    scratch += [pltpu.VMEM(x.shape, x.dtype) for x in operands[5:]]
    scratch += [pltpu.VMEM((tokens + 8, channels), F32) for _ in range(3)]
    scratch += [pltpu.VMEM((8, channels), F32) for _ in range(2)]
    scratch += [pltpu.VMEM((channels, tokens), BF16) for _ in range(2)]
    scratch += [pltpu.VMEM((2, channels, tokens // 2), BF16) for _ in range(4)]
    scratch += [pltpu.VMEM(block, BF16)]
    scratch += [pltpu.VMEM((channels, tokens), F32) for _ in range(3)]
    scratch += [
        pltpu.VMEM((tokens // LANES, channels + own, LANES), F32),
        pltpu.VMEM((own * LANES, 2 * LANES), F32),
        pltpu.VMEM((tokens // LANES // 2, channels + own, LANES), F32),
        pltpu.VMEM((groups, 1, tokens), F32),
    ]
    scratch += [pltpu.SemaphoreType.DMA((count,)) for count in (14, 2, 5, 5, 2)]
    anywhere = pl.BlockSpec(memory_space=pl.ANY)
    operands = tuple(pltpu.with_memory_space_constraint(x, pltpu.HBM) for x in operands)
    both = pl.pallas_call(
        functools.partial(kernel, pieces, groups),
        out_shape=jax.ShapeDtypeStruct((2, *block), BF16),
        in_specs=[anywhere] * len(operands),
        out_specs=pl.BlockSpec(memory_space=pltpu.VMEM),
        scratch_shapes=scratch,
        compiler_params=pltpu.CompilerParams(
            collective_id=0, has_side_effects=True, vmem_limit_bytes=32 * 2**20
        ),
        cost_estimate=pl.CostEstimate(flops=1_300_000_000, bytes_accessed=4_000_000, transcendentals=0),
    )(*operands)
    return both[0], both[1]


def solution(mesh):
    pieces = mesh.shape["seq"]
    constants = tuple(jnp.asarray(x) for x in tables(pieces))
    placed = (
        P("seq", "ch"),
        P("seq", "ch"),
        P("seq", "ch"),
        P(None, None, "ch"),
        P("seq", "ch"),
        P("ch"),
        P("seq", "ch"),
        P("ch"),
    )
    return jax.shard_map(
        functools.partial(per_device, constants),
        mesh=mesh,
        in_specs=placed,
        out_specs=(P("seq", "ch"), P("seq", "ch")),
        check_vma=False,
    )
```
